256 devices in a mesh: space: 128 (over y, z_lo, x, core), phase: 2 (over z_hi).
Axes of the slice: x: 4, y: 4, z: 8 (z_hi: 2, z_lo: 4; z = z_hi * 4 + z_lo), core: 2. Of those that a mesh axis runs over, the one named last changes fastest.
Arguments:
- particle_cell: int32 [2, 8192, 128], P('phase', 'space'), may hold values from 0 to 63
- block_count: int32 [2, 8192], P('phase', 'space'), may hold values from 1 to 128, as said below
- particle_frac: float32 [2, 3, 8192, 128], P('phase', None, 'space'), may hold values from 0 to 1
- particle_vel: float32 [2, 3, 8192, 128], P('phase', None, 'space'), may hold values from -2.5 to 2.5
- particle_mass: float32 [2, 8192, 128], P('phase', 'space'), may hold values from 0.5 to 2
- particle_stress: float32 [2, 8192, 128], P('phase', 'space'), may hold values from -6 to 6
- drag_coef: float32 [512, 8, 128], P('space'), may hold values from 0.2 to 5
Outputs:
- frac_out: float32 [2, 3, 8192, 128], P('phase', None, 'space')
- vel_out: float32 [2, 3, 8192, 128], P('phase', None, 'space')
- stress_out: float32 [2, 8192, 128], P('phase', 'space')
The draws below stay inside these ranges and needn't reach their ends.
Inputs may be any that keep to these rules, and one draw needn't show every extreme that they name: `particle_cell`: the cell of a slot within its block of 4 x 4 x 4 cells, numbered 16 a + 4 b + c for the offsets a, b, c along the first, second and third dimension. `block_count`: slots 0 to count - 1 of a block hold particles, the others are empty; among the blocks b with the same b // 64 in a phase, one has all 128 slots live.
All inputs are finite; a program needn't handle non-finite values.
Results may differ from the reference program's by a relative error of at most 0.0003.
Values sent between devices are 32-bit elements; how exact they have to be, the bound alone decides.
A program may use at most 64 MiB of HBM per device.

```python
import math
import jax
import jax.numpy as jnp
from jax import lax

NBY = 2
NBZ = 32
SLOTS = 128
OUTER = 1
SUBSTEPS = 2
NB = 64
BLOCKS = 8192
PHASES = 2
NX = 512
NY = 8
NZ = 128
N_SPACE = 128


def draw_block_count(key, part):
    base_key = jax.random.fold_in(key, 7177)
    level_key, count_key, full_key = jax.random.split(base_key, 3)
    ndevice = BLOCKS // NB
    level_shift = jax.random.randint(level_key, (PHASES, ndevice, 1), 0, 4)
    load_level = jnp.right_shift(jnp.full((PHASES, ndevice, 1), SLOTS, jnp.int32), level_shift)
    lowest = load_level // 2
    raw_draw = jax.random.randint(count_key, (PHASES, ndevice, NB), 0, 1 << 30)
    counts = lowest + raw_draw % (load_level - lowest + 1)
    full_block = jax.random.randint(full_key, (PHASES, ndevice, 1), 0, NB)
    block_ids = jnp.arange(NB, dtype=jnp.int32)[None, None, :]
    counts = jnp.where(block_ids == full_block, SLOTS, counts)
    return counts.reshape(PHASES, BLOCKS).astype(jnp.int32)


def place_ends(drawn, rng, smallest, top_value):
    longest = drawn.shape.index(max(drawn.shape))
    spots = []
    for shift in (0, 1):
        where = [jax.random.randint(jax.random.fold_in(rng, axis), (), 0, length) for axis, length in enumerate(drawn.shape)]
        where[longest] = (where[longest] + shift) % drawn.shape[longest]
        spots.append(tuple(where))
    return drawn.at[spots[0]].set(smallest).at[spots[1]].set(top_value)


def steps_of(rng, dims, shards, low, largest):
    factor_of, own = 1.0, jax.random.fold_in(rng, 6)
    for dim, parts in shards:
        steps = jnp.exp(jax.random.uniform(jax.random.fold_in(own, dim), (parts,), jnp.float32, low / len(shards), largest / len(shards)))
        factor_of = factor_of * jnp.repeat(steps, dims[dim] // parts).reshape([-1 if axis == dim else 1 for axis in range(len(dims))])
    return factor_of


def noise(rng, dims, deviation, bound, cuts=(), kind=jnp.bfloat16):
    level = steps_of(rng, dims, cuts, -0.22, 0.18) if cuts else 1.0
    values = jax.random.normal(rng, dims, jnp.float32) * deviation * level
    return jnp.minimum(jnp.maximum(values, -bound), bound).astype(kind)


def setup_inputs(seed: int = 0) -> dict:
    seeds = jax.random.split(jax.random.key(seed), 8)
    particle_cell = place_ends(jax.random.randint(seeds[0], (PHASES, BLOCKS, SLOTS), 0, 64), jax.random.fold_in(seeds[0], 1), 0, 63).astype(jnp.int32)
    block_count = draw_block_count(jax.random.fold_in(seeds[7], 71), 0)
    particle_frac = jnp.clip(1.0 * jax.random.uniform(seeds[2], (PHASES, 3, BLOCKS, SLOTS), jnp.float32) ** steps_of(seeds[2], (PHASES, 3, BLOCKS, SLOTS), ((0, 2), (2, 128)), -0.2, 0.2), 0.0, 1.0)
    particle_vel = noise(seeds[3], (PHASES, 3, BLOCKS, SLOTS), 0.5, 2.5, ((0, 2), (2, 128)), jnp.float32)
    particle_mass = jnp.clip(jnp.exp(math.log(2.0) - 1.3862944 * jax.random.uniform(seeds[4], (PHASES, BLOCKS, SLOTS), jnp.float32) ** steps_of(seeds[4], (PHASES, BLOCKS, SLOTS), ((0, 2), (1, 128)), -0.2, 0.2)), 0.5, 2.0)
    particle_stress = noise(seeds[5], (PHASES, BLOCKS, SLOTS), 1.0, 6.0, ((0, 2), (1, 128)), jnp.float32)
    drag_coef = jnp.clip(jnp.exp(math.log(5.0) - 3.218876 * jax.random.uniform(seeds[6], (NX, NY, NZ), jnp.float32) ** steps_of(seeds[6], (NX, NY, NZ), ((0, 128),), -0.2, 0.2)), 0.2, 5.0)
    return {"particle_cell": particle_cell, "block_count": block_count, "particle_frac": particle_frac, "particle_vel": particle_vel, "particle_mass": particle_mass, "particle_stress": particle_stress, "drag_coef": drag_coef}


time_step = 0.05
gravity = 1.0
bulk_modulus = 4.0
mass_floor = 0.25
slip_floor = 0.25
highest = lax.Precision.HIGHEST

def intersection_add(array, axis):
    moved_arr = jnp.moveaxis(array, (axis, axis + 1), (-2, -1))
    nblock = moved_arr.shape[-2]
    leading = moved_arr.shape[:-2]
    flat_pad = [(0, 0)] * len(leading)
    main_part = moved_arr[..., :4].reshape(leading + (4 * nblock,))
    main_part = jnp.pad(main_part, flat_pad + [(0, 2)])
    tail_part = jnp.pad(moved_arr[..., 4:], flat_pad + [(0, 0), (0, 2)])
    tail_part = tail_part.reshape(leading + (4 * nblock,))
    tail_part = jnp.pad(tail_part, flat_pad + [(4, 0)])[..., :4 * nblock + 2]
    return jnp.moveaxis(main_part + tail_part, -1, axis)

def cut_windows(array, axis):
    moved_arr = jnp.moveaxis(array, axis, -1)
    nblock = (moved_arr.shape[-1] - 2) // 4
    leading = moved_arr.shape[:-1]
    main_part = moved_arr[..., :4 * nblock].reshape(leading + (nblock, 4))
    tail_part = jnp.pad(moved_arr[..., 4:], [(0, 0)] * len(leading) + [(0, 2)])
    tail_part = tail_part.reshape(leading + (nblock, 4))[..., :2]
    tile_set = jnp.concatenate([main_part, tail_part], axis=-1)
    return jnp.moveaxis(tile_set, (-2, -1), (axis, axis + 1))

def axis_factors(offset, within):
    relative = within - 0.5
    weights = (0.5 * (0.5 - relative) * (0.5 - relative), 0.75 - relative * relative, 0.5 * (0.5 + relative) * (0.5 + relative))
    places = lax.broadcasted_iota(jnp.int32, (1, 6, 1), 1)
    result = jnp.zeros(offset.shape[:1] + (6,) + offset.shape[1:], within.dtype)
    for stencil, weight in enumerate(weights):
        result = result + jnp.where(places == offset[:, None, :] + stencil, weight[:, None, :], 0.0)
    return result

def particle_frame(cell_ids, frac_part, counts):
    nblocks, slot_count = cell_ids.shape
    is_live = lax.broadcasted_iota(jnp.int32, (nblocks, slot_count), 1) < counts[:, None]
    offset_x = cell_ids // 16
    offset_y = cell_ids // 4 % 4
    offset_z = cell_ids % 4
    block_ids = lax.broadcasted_iota(jnp.int32, (nblocks, slot_count), 0)
    start_y = 4 * (block_ids // NBZ)
    start_z = 4 * (block_ids % NBZ)
    position = jnp.stack([offset_x + frac_part[0], start_y + offset_y + frac_part[1], start_z + offset_z + frac_part[2]])
    return (is_live, (offset_x, offset_y, offset_z), position)

def node_coords(rows_y, rows_z, float_type):
    return (jnp.arange(6, dtype=float_type).reshape(6, 1, 1) - 0.5, jnp.arange(rows_y, dtype=float_type).reshape(1, rows_y, 1) + 0.5, jnp.arange(rows_z, dtype=float_type).reshape(1, 1, rows_z) + 0.5)

def plane_factors(offsets, frac_part):
    factor_x = axis_factors(offsets[0], frac_part[0])
    factor_y = axis_factors(offsets[1], frac_part[1])
    factor_z = axis_factors(offsets[2], frac_part[2])
    plane_xy = (factor_x[:, :, None] * factor_y[:, None]).reshape(factor_x.shape[0], 36, -1)
    return (plane_xy, factor_z)

def deposit(cell_ids, frac_part, velocity, node_mass_in, pressure, counts):
    is_live, offsets, position = particle_frame(cell_ids, frac_part, counts)
    mass_live = jnp.where(is_live, node_mass_in, 0.0)
    loaded = jnp.where(is_live, pressure, 0.0)
    channels = jnp.stack([mass_live, mass_live * velocity[0], mass_live * velocity[1], mass_live * velocity[2], loaded, loaded * position[0], loaded * position[1], loaded * position[2]], axis=1)
    plane_xy, factor_z = plane_factors(offsets, frac_part)
    column = (channels[:, :, None] * factor_z[:, None]).reshape(channels.shape[0], 48, -1)
    tile_set = jnp.einsum('gap,gmp->gam', plane_xy, column, precision=highest)
    tile_set = tile_set.reshape(NBY, NBZ, 6, 6, 8, 6).transpose(4, 2, 0, 3, 1, 5)
    summed = intersection_add(intersection_add(tile_set, 4), 2)[:, :, 1:-1, 1:-1]
    node_pos = node_coords(summed.shape[2], summed.shape[3], summed.dtype)
    momentum = [summed[1 + axis_id] + 4.0 * time_step * (node_pos[axis_id] * summed[4] - summed[5 + axis_id]) for axis_id in range(3)]
    return jnp.stack([summed[0]] + momentum)

def grid_velocity(fields):
    velocity = fields[1:4] / jnp.maximum(fields[0], mass_floor)
    lifted = velocity[2] - time_step * gravity
    floor_mask = lax.broadcasted_iota(jnp.int32, lifted.shape, 2) == 0
    lifted = jnp.where(floor_mask, jnp.maximum(lifted, 0.0), lifted)
    return jnp.stack([velocity[0], velocity[1], lifted])

def apply_drag(velocity, node_mass, other_velocity, other_mass, coefficient):
    slip_vel = other_velocity - velocity
    slip_speed = jnp.sqrt(lax.optimization_barrier(jnp.sum(slip_vel * slip_vel, axis=0)) + slip_floor)
    drag_rate = coefficient * slip_speed
    mass_share = other_mass / (node_mass + other_mass + mass_floor)
    return velocity + drag_rate / (1.0 + drag_rate) * mass_share * slip_vel

def gather_back(grid_vel, cell_ids, frac_part, velocity, pressure, counts):
    is_live, offsets, position = particle_frame(cell_ids, frac_part, counts)
    node_pos = node_coords(grid_vel.shape[2], grid_vel.shape[3], grid_vel.dtype)
    dotted = node_pos[0] * grid_vel[0] + node_pos[1] * grid_vel[1] + node_pos[2] * grid_vel[2]
    fields = jnp.concatenate([grid_vel, dotted[None]], axis=0)
    fields = jnp.pad(fields, ((0, 0), (0, 0), (1, 1), (1, 1)))
    tile_set = cut_windows(cut_windows(fields, 3), 2)
    tile_set = tile_set.transpose(2, 4, 1, 3, 0, 5).reshape(NBY * NBZ, 36, 24)
    plane_xy, factor_z = plane_factors(offsets, frac_part)
    spread = jnp.einsum('gam,gap->gmp', tile_set, plane_xy, precision=highest)
    spread = spread.reshape(tile_set.shape[0], 4, 6, -1)
    sampled = lax.optimization_barrier(jnp.sum(spread * factor_z[:, None], axis=2))
    sampled = jnp.moveaxis(sampled, 1, 0)
    new_vel = sampled[:3]
    spread_rate = 4.0 * (sampled[3] - lax.optimization_barrier(jnp.sum(position * new_vel, axis=0)))
    out_frac = jnp.where(is_live[None], frac_part + time_step * new_vel, frac_part)
    out_vel = jnp.where(is_live[None], new_vel, velocity)
    out_stress = jnp.where(is_live, pressure - time_step * bulk_modulus * spread_rate, pressure)
    return (out_frac, out_vel, out_stress)

def reference(particle_cell, block_count, particle_frac, particle_vel, particle_mass, particle_stress, drag_coef):
    nblock = NBY * NBZ
    cell_parts = [particle_cell[phase_id].reshape(N_SPACE, nblock, SLOTS) for phase_id in range(2)]
    count_parts = [block_count[phase_id].reshape(N_SPACE, nblock) for phase_id in range(2)]
    frac_parts = [jnp.moveaxis(particle_frac[phase_id].reshape(3, N_SPACE, nblock, SLOTS), 1, 0) for phase_id in range(2)]
    vel_parts = [jnp.moveaxis(particle_vel[phase_id].reshape(3, N_SPACE, nblock, SLOTS), 1, 0) for phase_id in range(2)]
    mass_parts = [particle_mass[phase_id].reshape(N_SPACE, nblock, SLOTS) for phase_id in range(2)]
    stress_parts = [particle_stress[phase_id].reshape(N_SPACE, nblock, SLOTS) for phase_id in range(2)]
    for outer_step in range(OUTER):
        for sub_step in range(SUBSTEPS):
            grid_list = []
            for phase_id in range(2):
                deposits = lax.map(lambda packed: deposit(packed[0], packed[1], packed[2], packed[3], packed[4], packed[5]), (cell_parts[phase_id], frac_parts[phase_id], vel_parts[phase_id], mass_parts[phase_id], stress_parts[phase_id], count_parts[phase_id]))
                fields = intersection_add(jnp.moveaxis(deposits, 0, 1), 1)[:, 1:-1]
                grid_list.append((fields[0], grid_velocity(fields)))
            if sub_step == 0:
                solid_vel = apply_drag(grid_list[0][1], grid_list[0][0], grid_list[1][1], grid_list[1][0], drag_coef)
                water_vel = apply_drag(grid_list[1][1], grid_list[1][0], grid_list[0][1], grid_list[0][0], drag_coef)
                velocities = [solid_vel, water_vel]
            else:
                velocities = [grid_list[0][1], grid_list[1][1]]
            for phase_id in range(2):
                padded = jnp.pad(velocities[phase_id], ((0, 0), (1, 1), (0, 0), (0, 0)))
                windows = jnp.moveaxis(cut_windows(padded, 1), 1, 0)
                new_state = lax.map(lambda packed: gather_back(packed[0], packed[1], packed[2], packed[3], packed[4], packed[5]), (windows, cell_parts[phase_id], frac_parts[phase_id], vel_parts[phase_id], stress_parts[phase_id], count_parts[phase_id]))
                frac_parts[phase_id] = new_state[0]
                vel_parts[phase_id] = new_state[1]
                stress_parts[phase_id] = new_state[2]
    frac_out = jnp.stack([jnp.moveaxis(frac_parts[phase_id], 0, 1).reshape(3, N_SPACE * nblock, SLOTS) for phase_id in range(2)])
    vel_out = jnp.stack([jnp.moveaxis(vel_parts[phase_id], 0, 1).reshape(3, N_SPACE * nblock, SLOTS) for phase_id in range(2)])
    stress_out = jnp.stack([stress_parts[phase_id].reshape(N_SPACE * nblock, SLOTS) for phase_id in range(2)])
    return (frac_out, vel_out, stress_out)
```

```python
import jax
import jax.numpy as jnp
from jax import lax
from jax.experimental import pallas as pl
from jax.experimental.pallas import tpu as pltpu
from jax.sharding import PartitionSpec as P

F32 = jnp.float32
BF16 = jnp.bfloat16
DT = 0.05
MESH = pl.DeviceIdType.MESH

FX, WY, WZ, MASS, QX, QY, QZ, S2 = 0, 6, 9, 12, 13, 14, 15, 16
NROW = 17


def split(value):
    high = value.astype(BF16)
    low = (value - high.astype(F32)).astype(BF16)
    return high, low


def factors(frac):
    r = frac - 0.5
    return 0.5 * (0.5 - r) * (0.5 - r), 0.75 - r * r, 0.5 * (0.5 + r) * (0.5 + r)


def kernel(
    cell_ref,
    count_ref,
    frac_in,
    vel_in,
    mass_ref,
    stress_in,
    drag_ref,
    frac_out,
    vel_out,
    stress_out,
    live_s,
    rows_s,
    base_s,
    ph_s,
    pl_s,
    fz_s,
    fzt_s,
    even_s,
    odd_s,
    vt_s,
    red_s,
    grid_s,
    edge_s,
    left_s,
    right_s,
    other_s,
    coef_s,
    send_sem,
    recv_sem,
):
    n_space = lax.axis_size("space")
    me = lax.axis_index("space")
    phase = lax.axis_index("phase")
    right = lax.rem(me + 1, n_space)
    left = lax.rem(me + n_space - 1, n_space)
    to_left = (left, phase)
    to_right = (right, phase)
    to_other = (me, 1 - phase)

    barrier = pltpu.get_barrier_semaphore()
    for target in (to_left, to_right, to_other):
        pl.semaphore_signal(barrier, inc=1, device_id=target, device_id_type=MESH)
    pl.semaphore_wait(barrier, 3)

    def remote(src, dst, sem, target):
        return pltpu.make_async_remote_copy(
            src_ref=src,
            dst_ref=dst,
            send_sem=send_sem.at[sem],
            recv_sem=recv_sem.at[sem],
            device_id=target,
            device_id_type=MESH,
        )

    coef_copies = (
        remote(drag_ref.at[0], coef_s.at[1], 0, to_left),
        remote(drag_ref.at[3], coef_s.at[0], 1, to_right),
    )
    for copy in coef_copies:
        copy.start()

    sub8 = lax.broadcasted_iota(jnp.int32, (8, 128), 0)
    zero8 = jnp.zeros((8, 128), F32)

    diagonal = lax.broadcasted_iota(jnp.int32, (64, 64), 0) == lax.broadcasted_iota(jnp.int32, (64, 64), 1)
    counts = jnp.broadcast_to(count_ref[...].astype(F32), (64, 64))
    counts = jnp.sum(jnp.where(diagonal, counts, 0.0), axis=1, keepdims=True)
    slots = lax.broadcasted_iota(jnp.int32, (64, 128), 1).astype(F32)
    live_s[...] = jnp.where(slots < counts, 1.0, 0.0)

    for c in range(5):
        even_s[c, 128:136, :] = zero8
        odd_s[c, 0:8, :] = zero8
    for c in range(4):
        vt_s[c, 0:8, :] = zero8
        vt_s[c, 136:144, :] = zero8

    def coords(j, frac):
        here = pl.ds(pl.multiple_of(8 * j, 8), 8)
        cell = cell_ref[here, :]
        cx = cell >> 4
        cy = (cell >> 2) & 3
        cz = cell & 3
        by = j // 4
        pos_x = cx.astype(F32) + (frac[0, here, :] - 2.0)
        pos_y = (cy + 4 * by).astype(F32) + (frac[1, here, :] - 4.0)
        return here, cx, cy, cz, by, pos_x, pos_y

    def prepare(frac, vel, stress):
        def body(j, carry):
            here, cx, cy, cz, by, pos_x, pos_y = coords(j, frac)
            wx = factors(frac[0, here, :])
            wy = factors(frac[1, here, :])
            wz = factors(frac[2, here, :])
            at = [cx == k for k in range(4)]
            for a in range(6):
                value = zero8
                for k in range(4):
                    if 0 <= a - k <= 2:
                        value = jnp.where(at[k], wx[a - k], value)
                rows_s[FX + a, here, :] = value
            for k in range(3):
                rows_s[WY + k, here, :] = wy[k]
                rows_s[WZ + k, here, :] = wz[k]
            base_s[0, here, :] = cy + (4 * by - 1)
            base_s[1, here, :] = (cz + 4 * (sub8 & 1) - 1) & 7
            live = live_s[here, :] > 0.5
            m = jnp.where(live, mass_ref[here, :], 0.0)
            s2 = jnp.where(live, stress[here, :], 0.0) * (4.0 * DT)
            rows_s[MASS, here, :] = m
            rows_s[S2, here, :] = s2
            rows_s[QX, here, :] = m * vel[0, here, :] - s2 * pos_x
            rows_s[QY, here, :] = m * vel[1, here, :] - s2 * pos_y
            rows_s[QZ, here, :] = m * vel[2, here, :] - s2 * (frac[2, here, :] - 0.5)
            return carry

        lax.fori_loop(0, 8, body, 0)

    def deposit():
        def body(i, carry):
            for par in range(2):
                bz = 2 * i + par
                plane = []
                column = []
                for by in range(2):
                    at = pl.ds(bz + 32 * by, 1)

                    def row(f):
                        return jnp.broadcast_to(rows_s[f, at, :], (8, 128))

                    t = sub8 - jnp.broadcast_to(base_s[0, at, :], (8, 128))
                    fy = jnp.where(t == 0, row(WY), jnp.where(t == 1, row(WY + 1), jnp.where(t == 2, row(WY + 2), 0.0)))
                    t = (sub8 - jnp.broadcast_to(base_s[1, at, :], (8, 128))) & 7
                    fz = jnp.where(t == 0, row(WZ), jnp.where(t == 1, row(WZ + 1), jnp.where(t == 2, row(WZ + 2), 0.0)))
                    tm1 = (t - 1).astype(F32)
                    s2 = row(S2)
                    plane.append(jnp.concatenate([row(FX + a) * fy for a in range(6)], axis=0))
                    column.append(
                        jnp.concatenate(
                            [
                                row(MASS) * fz,
                                row(QX) * fz,
                                row(QY) * fz,
                                (row(QZ) + s2 * tm1) * fz,
                                s2 * fz,
                            ],
                            axis=0,
                        )
                    )
                    here = pl.ds(pl.multiple_of(8 * bz, 8), 8)
                    fz_s[by, here, :] = fz
                    fzt_s[by, here, :] = fz * tm1
                plane_hi, plane_lo = split(jnp.concatenate(plane, axis=1))
                ph_s[bz] = plane_hi
                pl_s[bz] = plane_lo
                column_hi, column_lo = split(jnp.concatenate(column, axis=1))
                out = lax.dot_general(
                    jnp.concatenate([column_hi, column_lo], axis=0),
                    jnp.concatenate([plane_hi, plane_lo, jnp.zeros((32, 256), BF16)], axis=0),
                    (((1,), (1,)), ((), ())),
                    preferred_element_type=F32,
                )
                out = out[:40] + out[40:]
                for c in range(5):
                    if par == 0:
                        even_s[c, pl.ds(pl.multiple_of(8 * i, 8), 8), :] = out[8 * c : 8 * c + 8]
                    else:
                        odd_s[c, pl.ds(pl.multiple_of(8 * i + 8, 8), 8), :] = out[8 * c : 8 * c + 8]
            return carry

        lax.fori_loop(0, 16, body, 0)
        fields = []
        row7 = (lax.broadcasted_iota(jnp.int32, (128, 128), 0) & 7) == 7
        row0 = (lax.broadcasted_iota(jnp.int32, (128, 128), 0) & 7) == 0
        for c in range(5):
            total = jnp.where(row7, even_s[c, 8:136, :], even_s[c, 0:128, :]) + jnp.where(
                row0, odd_s[c, 0:128, :], odd_s[c, 8:136, :]
            )
            turned = total.T
            fields.append((turned[0:48] + turned[48:96]).reshape(6, 8, 128))
        y = lax.broadcasted_iota(jnp.int32, (8, 128), 0).astype(F32) - 3.5
        for a in range(6):
            grid_s[a, 0] = fields[0][a]
            grid_s[a, 1] = fields[1][a] + (a - 2.5) * fields[4][a]
            grid_s[a, 2] = fields[2][a] + y * fields[4][a]
            grid_s[a, 3] = fields[3][a]

    floor = lax.broadcasted_iota(jnp.int32, (8, 128), 1) == 0

    def velocity(mass, momentum):
        inverse = 1.0 / jnp.maximum(mass, 0.25)
        v = [momentum[e] * inverse for e in range(3)]
        v[2] = v[2] - DT
        v[2] = jnp.where(floor, jnp.maximum(v[2], 0.0), v[2])
        return v

    def gather(node_vel, frac, vel, stress):
        y = lax.broadcasted_iota(jnp.int32, (8, 128), 0).astype(F32) - 3.5
        for c in range(4):
            if c < 3:
                values = [node_vel[a][c] for a in range(6)]
            else:
                values = [(a - 2.5) * node_vel[a][0] + y * node_vel[a][1] for a in range(6)]
            values = jnp.concatenate(values, axis=0)
            high = values.astype(BF16).astype(F32)
            turned = jnp.concatenate([high, values - high, jnp.zeros((32, 128), F32)], axis=0).T
            vt_s[c, 8:136, :] = turned

        def body(i, carry):
            for par in range(2):
                bz = 2 * i + par
                window = []
                for c in range(4):
                    here = vt_s[c, pl.ds(pl.multiple_of(8 * i + 8, 8), 8), :]
                    if par == 0:
                        beside = vt_s[c, pl.ds(pl.multiple_of(8 * i, 8), 8), :]
                        window.append(jnp.where(sub8 == 7, beside, here))
                    else:
                        beside = vt_s[c, pl.ds(pl.multiple_of(8 * i + 16, 8), 8), :]
                        window.append(jnp.where(sub8 == 0, beside, here))
                window = jnp.concatenate(window, axis=0).astype(BF16)
                high, low, none = ph_s[bz], pl_s[bz], jnp.zeros((32, 256), BF16)
                out = jnp.dot(
                    jnp.concatenate([window, window], axis=1),
                    jnp.concatenate([high, high, none, low, low, none], axis=0),
                    preferred_element_type=F32,
                )
                at = pl.ds(pl.multiple_of(8 * bz, 8), 8)
                for by in range(2):
                    fz, fzt = fz_s[by, at, :], fzt_s[by, at, :]
                    u = [out[8 * c : 8 * c + 8, 128 * by : 128 * by + 128] for c in range(4)]
                    for c in range(3):
                        red_s[2 * c + by, at, :] = fz * u[c]
                    red_s[6 + by, at, :] = fz * u[3] + fzt * u[2]
            return carry

        lax.fori_loop(0, 16, body, 0)

        for j in range(8):
            here, cx, cy, cz, by, pos_x, pos_y = coords(j, frac)
            sums = []
            for c in range(4):
                value = red_s[2 * c + by, pl.ds(64 * (j % 4), 8, stride=8), :]
                for s in range(1, 8):
                    value = value + red_s[2 * c + by, pl.ds(64 * (j % 4) + s, 8, stride=8), :]
                sums.append(value)
            live = live_s[here, :] > 0.5
            rate = sums[3] - pos_x * sums[0] - pos_y * sums[1] - (frac[2, here, :] - 0.5) * sums[2]
            stress_out[here, :] = stress[here, :] - jnp.where(live, (4.0 * 4.0 * DT) * rate, 0.0)
            for e in range(3):
                f = frac[e, here, :]
                frac_out[e, here, :] = jnp.where(live, f + DT * sums[e], f)
                vel_out[e, here, :] = jnp.where(live, sums[e], vel[e, here, :])

    first = me == 0
    last = me == n_space - 1

    for step in range(2):
        frac, vel, stress = (frac_in, vel_in, stress_in) if step == 0 else (frac_out, vel_out, stress_out)
        prepare(frac, vel, stress)
        deposit()
        copies = [
            remote(grid_s.at[0:2], right_s.at[step], 2 + 2 * step, to_left),
            remote(grid_s.at[4:6], left_s.at[step], 3 + 2 * step, to_right),
        ]
        for copy in copies:
            copy.start()
        if step == 0:
            inner = remote(grid_s.at[2:4], other_s.at[2:4], 6, to_other)
            inner.start()
        for copy in copies:
            copy.wait()
        for a in range(2):
            for c in range(4):
                edge_s[a, c] = grid_s[a, c] + jnp.where(first, 0.0, left_s[step, a, c])
                edge_s[2 + a, c] = grid_s[4 + a, c] + jnp.where(last, 0.0, right_s[step, a, c])
        if step == 0:
            outer = [
                remote(edge_s.at[0:2], other_s.at[0:2], 7, to_other),
                remote(edge_s.at[2:4], other_s.at[4:6], 8, to_other),
            ]
            for copy in outer:
                copy.start()
        full = []
        for a in range(6):
            if a < 2:
                full.append([edge_s[a, c] for c in range(4)])
            elif a < 4:
                full.append([grid_s[a, c] for c in range(4)])
            else:
                full.append([edge_s[a - 2, c] for c in range(4)])
        node_vel = [velocity(f[0], f[1:]) for f in full]
        if step == 0:
            for copy in coef_copies + (inner,) + tuple(outer):
                copy.wait()
            for a in range(6):
                mass = full[a][0]
                other_mass = other_s[a, 0]
                other_vel = velocity(other_mass, [other_s[a, c] for c in range(1, 4)])
                coef = coef_s[0] if a == 0 else coef_s[1] if a == 5 else drag_ref[a - 1]
                slip = [other_vel[e] - node_vel[a][e] for e in range(3)]
                rate = coef * jnp.sqrt(slip[0] * slip[0] + slip[1] * slip[1] + slip[2] * slip[2] + 0.25)
                gain = rate / (1.0 + rate) * (other_mass / (mass + other_mass + 0.25))
                node_vel[a] = [node_vel[a][e] + gain * slip[e] for e in range(3)]
        node_vel[0] = [jnp.where(first, 0.0, v) for v in node_vel[0]]
        node_vel[5] = [jnp.where(last, 0.0, v) for v in node_vel[5]]
        gather(node_vel, frac, vel, stress)


def local(cell, count, frac, vel, mass, stress, drag):
    whole = pl.BlockSpec(memory_space=pltpu.VMEM)
    frac_out, vel_out, stress_out = pl.pallas_call(
        kernel,
        out_shape=(
            jax.ShapeDtypeStruct((3, 64, 128), F32),
            jax.ShapeDtypeStruct((3, 64, 128), F32),
            jax.ShapeDtypeStruct((64, 128), F32),
        ),
        in_specs=[whole] * 7,
        out_specs=(whole,) * 3,
        scratch_shapes=[
            pltpu.VMEM((64, 128), F32),
            pltpu.VMEM((NROW, 64, 128), F32),
            pltpu.VMEM((2, 64, 128), jnp.int32),
            pltpu.VMEM((32, 48, 256), BF16),
            pltpu.VMEM((32, 48, 256), BF16),
            pltpu.VMEM((2, 256, 128), F32),
            pltpu.VMEM((2, 256, 128), F32),
            pltpu.VMEM((5, 136, 128), F32),
            pltpu.VMEM((5, 136, 128), F32),
            pltpu.VMEM((4, 144, 128), F32),
            pltpu.VMEM((8, 256, 128), F32),
            pltpu.VMEM((6, 4, 8, 128), F32),
            pltpu.VMEM((4, 4, 8, 128), F32),
            pltpu.VMEM((2, 2, 4, 8, 128), F32),
            pltpu.VMEM((2, 2, 4, 8, 128), F32),
            pltpu.VMEM((6, 4, 8, 128), F32),
            pltpu.VMEM((2, 8, 128), F32),
            pltpu.SemaphoreType.DMA((9,)),
            pltpu.SemaphoreType.DMA((9,)),
        ],
        compiler_params=pltpu.CompilerParams(
            collective_id=0, has_side_effects=True, vmem_limit_bytes=32 * 1024 * 1024
        ),
    )(cell[0], count, frac[0], vel[0], mass[0], stress[0], drag)
    return frac_out[None], vel_out[None], stress_out[None]


def solution(mesh):
    in_specs = (
        P("phase", "space", None),
        P("phase", "space"),
        P("phase", None, "space", None),
        P("phase", None, "space", None),
        P("phase", "space", None),
        P("phase", "space", None),
        P("space", None, None),
    )
    out_specs = (
        P("phase", None, "space", None),
        P("phase", None, "space", None),
        P("phase", "space", None),
    )
    return jax.shard_map(local, mesh=mesh, in_specs=in_specs, out_specs=out_specs, check_vma=False)
```

```python
import jax
import jax.numpy as jnp
from jax import lax
from jax.experimental import pallas as pl
from jax.experimental.pallas import tpu as pltpu
from jax.sharding import PartitionSpec as P

F32 = jnp.float32
BF16 = jnp.bfloat16
DT = 0.05
MESH = pl.DeviceIdType.MESH

FX, WY, WZ, MASS, QX, QY, QZ, S2 = 0, 6, 9, 12, 13, 14, 15, 16
NROW = 17


def split(value):
    high = value.astype(BF16)
    low = (value - high.astype(F32)).astype(BF16)
    return high, low


def factors(frac):
    r = frac - 0.5
    return 0.5 * (0.5 - r) * (0.5 - r), 0.75 - r * r, 0.5 * (0.5 + r) * (0.5 + r)


def coords(cell_ref, frac, j):
    here = pl.ds(8 * j, 8)
    cell = cell_ref[here, :]
    cx = cell >> 4
    cy = (cell >> 2) & 3
    cz = cell & 3
    by = j // 4
    pos_x = cx.astype(F32) + (frac[0, here, :] - 2.0)
    pos_y = (cy + 4 * by).astype(F32) + (frac[1, here, :] - 4.0)
    return here, cx, cy, cz, by, pos_x, pos_y


def gather(vt_s, ph_s, pl_s, fz_s, fzt_s, red_s, cell_ref, live_s, state, out):
    frac, vel, stress = state
    frac_out, vel_out, stress_out = out
    sub8 = lax.broadcasted_iota(jnp.int32, (8, 128), 0)

    def body(i, carry):
        for par in range(2):
            bz = 2 * i + par
            window = []
            for c in range(4):
                here = vt_s[c, pl.ds(pl.multiple_of(8 * i + 8, 8), 8), :]
                if par == 0:
                    beside = vt_s[c, pl.ds(pl.multiple_of(8 * i, 8), 8), :]
                    window.append(jnp.where(sub8 == 7, beside, here))
                else:
                    beside = vt_s[c, pl.ds(pl.multiple_of(8 * i + 16, 8), 8), :]
                    window.append(jnp.where(sub8 == 0, beside, here))
            window = jnp.concatenate(window, axis=0).astype(BF16)
            high, low, none = ph_s[bz], pl_s[bz], jnp.zeros((32, 256), BF16)
            got = jnp.dot(
                jnp.concatenate([window, window], axis=1),
                jnp.concatenate([high, high, none, low, low, none], axis=0),
                preferred_element_type=F32,
            )
            at = pl.ds(pl.multiple_of(8 * bz, 8), 8)
            for by in range(2):
                fz, fzt = fz_s[by, at, :], fzt_s[by, at, :]
                u = [got[8 * c : 8 * c + 8, 128 * by : 128 * by + 128] for c in range(4)]
                for c in range(3):
                    red_s[2 * c + by, at, :] = fz * u[c]
                red_s[6 + by, at, :] = fz * u[3] + fzt * u[2]
        return carry

    lax.fori_loop(0, 16, body, 0, unroll=16)

    for j in range(8):
        here, cx, cy, cz, by, pos_x, pos_y = coords(cell_ref, frac, j)
        sums = []
        for c in range(4):
            parts = [red_s[2 * c + by, pl.ds(64 * (j % 4) + s, 8, stride=8), :] for s in range(8)]
            while len(parts) > 1:
                parts = [parts[k] + parts[k + 1] for k in range(0, len(parts), 2)]
            sums.append(parts[0])
        live = live_s[here, :] > 0.5
        rate = sums[3] - pos_x * sums[0] - pos_y * sums[1] - (frac[2, here, :] - 0.5) * sums[2]
        stress_out[here, :] = stress[here, :] - jnp.where(live, (4.0 * 4.0 * DT) * rate, 0.0)
        for e in range(3):
            f = frac[e, here, :]
            frac_out[e, here, :] = jnp.where(live, f + DT * sums[e], f)
            vel_out[e, here, :] = jnp.where(live, sums[e], vel[e, here, :])


def nodes_kernel(
    cell_hbm,
    count_hbm,
    frac_hbm,
    vel_hbm,
    mass_hbm,
    stress_hbm,
    drag_hbm,
    cell_ref,
    live_s,
    frac_mid,
    vel_mid,
    stress_mid,
    ph_s,
    pl_s,
    fz_s,
    fzt_s,
    vt_s,
    count_ref,
    frac_in,
    vel_in,
    mass_ref,
    stress_in,
    drag_ref,
    rows_s,
    base_s,
    even_s,
    odd_s,
    red_s,
    grid_s,
    left_s,
    right_s,
    cross_left_s,
    cross_right_s,
    other_s,
    load_sem,
    send_sem,
    recv_sem,
):
    n_space = lax.axis_size("space")
    me = lax.axis_index("space")
    phase = lax.axis_index("phase")
    right = lax.rem(me + 1, n_space)
    left = lax.rem(me + n_space - 1, n_space)
    to_left = (left, phase)
    to_right = (right, phase)
    to_other = (me, 1 - phase)
    to_cross_left = (left, 1 - phase)
    to_cross_right = (right, 1 - phase)

    barrier = pltpu.get_barrier_semaphore()
    for target in (to_left, to_right, to_other, to_cross_left, to_cross_right):
        pl.semaphore_signal(barrier, inc=1, device_id=target, device_id_type=MESH)

    loads = [
        pltpu.make_async_copy(src, dst, load_sem.at[k])
        for k, (src, dst) in enumerate(
            (
                (frac_hbm, frac_in),
                (cell_hbm, cell_ref),
                (count_hbm, count_ref),
                (vel_hbm, vel_in),
                (mass_hbm, mass_ref),
                (stress_hbm, stress_in),
                (drag_hbm, drag_ref),
            )
        )
    ]
    for load in loads:
        load.start()

    def remote(src, dst, sem, target):
        return pltpu.make_async_remote_copy(
            src_ref=src,
            dst_ref=dst,
            send_sem=send_sem.at[sem],
            recv_sem=recv_sem.at[sem],
            device_id=target,
            device_id_type=MESH,
        )

    sub8 = lax.broadcasted_iota(jnp.int32, (8, 128), 0)
    zero8 = jnp.zeros((8, 128), F32)
    for c in range(5):
        even_s[c, 128:136, :] = zero8
        odd_s[c, 0:8, :] = zero8
    for c in range(4):
        vt_s[c, 0:8, :] = zero8
        vt_s[c, 136:144, :] = zero8

    for load in loads:
        load.wait()

    diagonal = lax.broadcasted_iota(jnp.int32, (64, 64), 0) == lax.broadcasted_iota(jnp.int32, (64, 64), 1)
    counts = jnp.broadcast_to(count_ref[...].astype(F32), (64, 64))
    counts = jnp.sum(jnp.where(diagonal, counts, 0.0), axis=1, keepdims=True)
    slots = lax.broadcasted_iota(jnp.int32, (64, 128), 1).astype(F32)
    live_s[...] = jnp.where(slots < counts, 1.0, 0.0)

    def prepare(frac, vel, stress):
        for j in range(8):
            here, cx, cy, cz, by, pos_x, pos_y = coords(cell_ref, frac, j)
            wx = factors(frac[0, here, :])
            wy = factors(frac[1, here, :])
            wz = factors(frac[2, here, :])
            at = [cx == k for k in range(4)]
            for a in range(6):
                value = zero8
                for k in range(4):
                    if 0 <= a - k <= 2:
                        value = jnp.where(at[k], wx[a - k], value)
                rows_s[FX + a, here, :] = value
            for k in range(3):
                rows_s[WY + k, here, :] = wy[k]
                rows_s[WZ + k, here, :] = wz[k]
            base_s[0, here, :] = cy + (4 * by - 1)
            base_s[1, here, :] = (cz + 4 * (sub8 & 1) - 1) & 7
            live = live_s[here, :] > 0.5
            m = jnp.where(live, mass_ref[here, :], 0.0)
            s2 = jnp.where(live, stress[here, :], 0.0) * (4.0 * DT)
            rows_s[MASS, here, :] = m
            rows_s[S2, here, :] = s2
            rows_s[QX, here, :] = m * vel[0, here, :] - s2 * pos_x
            rows_s[QY, here, :] = m * vel[1, here, :] - s2 * pos_y
            rows_s[QZ, here, :] = m * vel[2, here, :] - s2 * (frac[2, here, :] - 0.5)

    def deposit(step):
        def body(i, carry):
            for par in range(2):
                bz = 2 * i + par
                plane = []
                column = []
                for by in range(2):
                    at = pl.ds(bz + 32 * by, 1)

                    def row(f):
                        return jnp.broadcast_to(rows_s[f, at, :], (8, 128))

                    t = sub8 - jnp.broadcast_to(base_s[0, at, :], (8, 128))
                    fy = jnp.where(t == 0, row(WY), jnp.where(t == 1, row(WY + 1), jnp.where(t == 2, row(WY + 2), 0.0)))
                    t = (sub8 - jnp.broadcast_to(base_s[1, at, :], (8, 128))) & 7
                    fz = jnp.where(t == 0, row(WZ), jnp.where(t == 1, row(WZ + 1), jnp.where(t == 2, row(WZ + 2), 0.0)))
                    tm1 = (t - 1).astype(F32)
                    s2 = row(S2)
                    plane.append(jnp.concatenate([row(FX + a) * fy for a in range(6)], axis=0))
                    column.append(
                        jnp.concatenate(
                            [
                                row(MASS) * fz,
                                row(QX) * fz,
                                row(QY) * fz,
                                (row(QZ) + s2 * tm1) * fz,
                                s2 * fz,
                            ],
                            axis=0,
                        )
                    )
                    here = pl.ds(pl.multiple_of(8 * bz, 8), 8)
                    fz_s[by, here, :] = fz
                    fzt_s[by, here, :] = fz * tm1
                plane_hi, plane_lo = split(jnp.concatenate(plane, axis=1))
                ph_s[bz] = plane_hi
                pl_s[bz] = plane_lo
                column_hi, column_lo = split(jnp.concatenate(column, axis=1))
                out = lax.dot_general(
                    jnp.concatenate([column_hi, column_lo], axis=0),
                    jnp.concatenate([plane_hi, plane_lo, jnp.zeros((32, 256), BF16)], axis=0),
                    (((1,), (1,)), ((), ())),
                    preferred_element_type=F32,
                )
                out = out[:40] + out[40:]
                for c in range(5):
                    if par == 0:
                        even_s[c, pl.ds(pl.multiple_of(8 * i, 8), 8), :] = out[8 * c : 8 * c + 8]
                    else:
                        odd_s[c, pl.ds(pl.multiple_of(8 * i + 8, 8), 8), :] = out[8 * c : 8 * c + 8]
            return carry

        lax.fori_loop(0, 16, body, 0, unroll=16)
        fields = []
        row7 = (lax.broadcasted_iota(jnp.int32, (128, 128), 0) & 7) == 7
        row0 = (lax.broadcasted_iota(jnp.int32, (128, 128), 0) & 7) == 0
        for c in range(5):
            total = jnp.where(row7, even_s[c, 8:136, :], even_s[c, 0:128, :]) + jnp.where(
                row0, odd_s[c, 0:128, :], odd_s[c, 8:136, :]
            )
            turned = total.T
            fields.append((turned[0:48] + turned[48:96]).reshape(6, 8, 128))
        y = sub8.astype(F32) - 3.5
        for a in range(6):
            grid_s[step, a, 0] = fields[0][a]
            grid_s[step, a, 1] = fields[1][a] + (a - 2.5) * fields[4][a]
            grid_s[step, a, 2] = fields[2][a] + y * fields[4][a]
            grid_s[step, a, 3] = fields[3][a]

    floor = lax.broadcasted_iota(jnp.int32, (8, 128), 1) == 0

    def velocity(mass, momentum):
        inverse = 1.0 / jnp.maximum(mass, 0.25)
        v = [momentum[e] * inverse for e in range(3)]
        v[2] = v[2] - DT
        v[2] = jnp.where(floor, jnp.maximum(v[2], 0.0), v[2])
        return v

    def turn(node_vel):
        y = sub8.astype(F32) - 3.5
        for c in range(4):
            if c < 3:
                values = [node_vel[a][c] for a in range(6)]
            else:
                values = [(a - 2.5) * node_vel[a][0] + y * node_vel[a][1] for a in range(6)]
            values = jnp.concatenate(values, axis=0)
            high = values.astype(BF16).astype(F32)
            turned = jnp.concatenate([high, values - high, jnp.zeros((32, 128), F32)], axis=0).T
            vt_s[c, 8:136, :] = turned

    first = me == 0
    last = me == n_space - 1
    started = []

    def settled(a, c, mine, from_left, from_right):
        if a < 2:
            return mine[a, c] + jnp.where(first, 0.0, from_left[a, c])
        if a < 4:
            return mine[a, c]
        return mine[a, c] + jnp.where(last, 0.0, from_right[a - 4, c])

    for step in range(2):
        state = (frac_in, vel_in, stress_in) if step == 0 else (frac_mid, vel_mid, stress_mid)
        prepare(*state)
        deposit(step)
        mine = grid_s.at[step]
        if step == 0:
            for a in range(1, 5):
                mine[a, 4] = drag_ref[a - 1]
            mine[0, 4] = zero8
            mine[5, 4] = zero8
            pl.semaphore_wait(barrier, 5)
            copies = [
                remote(mine.at[0:2], right_s.at[step], 0, to_left),
                remote(mine.at[4:6], left_s.at[step], 1, to_right),
                remote(mine.at[0:2, 0:4], cross_right_s, 2, to_cross_left),
                remote(mine.at[4:6, 0:4], cross_left_s, 3, to_cross_right),
                remote(mine.at[:, 0:4], other_s, 4, to_other),
            ]
        else:
            copies = [
                remote(mine.at[0:2, 0:4], right_s.at[step, :, 0:4], 5, to_left),
                remote(mine.at[4:6, 0:4], left_s.at[step, :, 0:4], 6, to_right),
            ]
        for copy in copies:
            copy.start()
        for copy in copies:
            copy.wait_recv()
        started += copies
        node_vel = []
        for a in range(6):
            full = [settled(a, c, mine, left_s.at[step], right_s.at[step]) for c in range(4)]
            v = velocity(full[0], full[1:])
            if step == 0:
                other = [settled(a, c, other_s, cross_left_s, cross_right_s) for c in range(4)]
                other_vel = velocity(other[0], other[1:])
                coef = left_s[0, 0, 4] if a == 0 else right_s[0, 1, 4] if a == 5 else drag_ref[a - 1]
                slip = [other_vel[e] - v[e] for e in range(3)]
                rate = coef * jnp.sqrt(slip[0] * slip[0] + slip[1] * slip[1] + slip[2] * slip[2] + 0.25)
                gain = rate / (1.0 + rate) * (other[0] / (full[0] + other[0] + 0.25))
                v = [v[e] + gain * slip[e] for e in range(3)]
            if a == 0:
                v = [jnp.where(first, 0.0, value) for value in v]
            if a == 5:
                v = [jnp.where(last, 0.0, value) for value in v]
            node_vel.append(v)
        turn(node_vel)
        if step == 0:
            gather(
                vt_s, ph_s, pl_s, fz_s, fzt_s, red_s, cell_ref, live_s, state, (frac_mid, vel_mid, stress_mid)
            )
    for copy in started:
        copy.wait_send()


def particles_kernel(
    cell_ref,
    live_s,
    frac_mid,
    vel_mid,
    stress_mid,
    ph_s,
    pl_s,
    fz_s,
    fzt_s,
    vt_s,
    frac_hbm,
    vel_hbm,
    stress_hbm,
    frac_out,
    vel_out,
    stress_out,
    red_s,
    store_sem,
):
    gather(
        vt_s,
        ph_s,
        pl_s,
        fz_s,
        fzt_s,
        red_s,
        cell_ref,
        live_s,
        (frac_mid, vel_mid, stress_mid),
        (frac_out, vel_out, stress_out),
    )
    stores = [
        pltpu.make_async_copy(src, dst, store_sem.at[k])
        for k, (src, dst) in enumerate(((frac_out, frac_hbm), (vel_out, vel_hbm), (stress_out, stress_hbm)))
    ]
    for store in stores:
        store.start()
    for store in stores:
        store.wait()


def local(cell, count, frac, vel, mass, stress, drag):
    vmem = pl.BlockSpec(memory_space=pltpu.VMEM)
    anywhere = pl.BlockSpec(memory_space=pl.ANY)
    passed = [
        ((64, 128), jnp.int32),
        ((64, 128), F32),
        ((3, 64, 128), F32),
        ((3, 64, 128), F32),
        ((64, 128), F32),
        ((32, 48, 256), BF16),
        ((32, 48, 256), BF16),
        ((2, 256, 128), F32),
        ((2, 256, 128), F32),
        ((4, 144, 128), F32),
    ]
    state = pl.pallas_call(
        nodes_kernel,
        out_shape=[jax.ShapeDtypeStruct(shape, kind) for shape, kind in passed],
        in_specs=[anywhere] * 7,
        out_specs=[vmem] * len(passed),
        scratch_shapes=[
            pltpu.VMEM((1, 64), jnp.int32),
            pltpu.VMEM((3, 64, 128), F32),
            pltpu.VMEM((3, 64, 128), F32),
            pltpu.VMEM((64, 128), F32),
            pltpu.VMEM((64, 128), F32),
            pltpu.VMEM((4, 8, 128), F32),
            pltpu.VMEM((NROW, 64, 128), F32),
            pltpu.VMEM((2, 64, 128), jnp.int32),
            pltpu.VMEM((5, 136, 128), F32),
            pltpu.VMEM((5, 136, 128), F32),
            pltpu.VMEM((8, 256, 128), F32),
            pltpu.VMEM((2, 6, 5, 8, 128), F32),
            pltpu.VMEM((2, 2, 5, 8, 128), F32),
            pltpu.VMEM((2, 2, 5, 8, 128), F32),
            pltpu.VMEM((2, 4, 8, 128), F32),
            pltpu.VMEM((2, 4, 8, 128), F32),
            pltpu.VMEM((6, 4, 8, 128), F32),
            pltpu.SemaphoreType.DMA((7,)),
            pltpu.SemaphoreType.DMA((7,)),
            pltpu.SemaphoreType.DMA((7,)),
        ],
        compiler_params=pltpu.CompilerParams(
            collective_id=0, has_side_effects=True, vmem_limit_bytes=24 * 1024 * 1024
        ),
    )(*[pltpu.with_memory_space_constraint(x, pltpu.HBM) for x in (cell[0], count, frac[0], vel[0], mass[0], stress[0], drag)])
    frac_out, vel_out, stress_out = pl.pallas_call(
        particles_kernel,
        out_shape=[
            jax.ShapeDtypeStruct((3, 64, 128), F32),
            jax.ShapeDtypeStruct((3, 64, 128), F32),
            jax.ShapeDtypeStruct((64, 128), F32),
        ],
        in_specs=[vmem] * len(passed),
        out_specs=[anywhere] * 3,
        scratch_shapes=[
            pltpu.VMEM((3, 64, 128), F32),
            pltpu.VMEM((3, 64, 128), F32),
            pltpu.VMEM((64, 128), F32),
            pltpu.VMEM((8, 256, 128), F32),
            pltpu.SemaphoreType.DMA((3,)),
        ],
        compiler_params=pltpu.CompilerParams(vmem_limit_bytes=24 * 1024 * 1024),
    )(*state)
    return frac_out[None], vel_out[None], stress_out[None]


def solution(mesh):
    in_specs = (
        P("phase", "space", None),
        P("phase", "space"),
        P("phase", None, "space", None),
        P("phase", None, "space", None),
        P("phase", "space", None),
        P("phase", "space", None),
        P("space", None, None),
    )
    out_specs = (
        P("phase", None, "space", None),
        P("phase", None, "space", None),
        P("phase", "space", None),
    )
    return jax.shard_map(local, mesh=mesh, in_specs=in_specs, out_specs=out_specs, check_vma=False)
```

```python
import jax
import jax.numpy as jnp
from jax import lax
from jax.experimental import pallas as pl
from jax.experimental.pallas import tpu as pltpu
from jax.sharding import PartitionSpec as P

F32 = jnp.float32
BF16 = jnp.bfloat16
DT = 0.05
MESH = pl.DeviceIdType.MESH
RUN = 32

FX, WY, WZ, MASS, QX, QY, QZ, S2 = 0, 6, 9, 12, 13, 14, 15, 16
NROW = 17


def split(value):
    high = value.astype(BF16)
    low = (value - high.astype(F32)).astype(BF16)
    return high, low


def factors(frac):
    r = frac - 0.5
    return 0.5 * (0.5 - r) * (0.5 - r), 0.75 - r * r, 0.5 * (0.5 + r) * (0.5 + r)


def coords(cell_ref, frac, j):
    here = pl.ds(8 * j, 8)
    cell = cell_ref[here, :]
    cx = cell >> 4
    cy = (cell >> 2) & 3
    cz = cell & 3
    by = j // 4
    pos_x = cx.astype(F32) + (frac[0, here, :] - 2.0)
    pos_y = (cy + 4 * by).astype(F32) + (frac[1, here, :] - 4.0)
    return here, cx, cy, cz, by, pos_x, pos_y


def gather(vt_s, ph_s, pl_s, fz_s, fzt_s, red_s, cell_ref, live_s, state, out):
    frac, vel, stress = state
    frac_out, vel_out, stress_out = out
    sub8 = lax.broadcasted_iota(jnp.int32, (8, 128), 0)

    def body(i, carry):
        for par in range(2):
            bz = 2 * i + par
            window = []
            for c in range(4):
                here = vt_s[c, pl.ds(pl.multiple_of(8 * i + 8, 8), 8), :]
                if par == 0:
                    beside = vt_s[c, pl.ds(pl.multiple_of(8 * i, 8), 8), :]
                    window.append(jnp.where(sub8 == 7, beside, here))
                else:
                    beside = vt_s[c, pl.ds(pl.multiple_of(8 * i + 16, 8), 8), :]
                    window.append(jnp.where(sub8 == 0, beside, here))
            window = jnp.concatenate(window, axis=0).astype(BF16)
            high, low, none = ph_s[bz], pl_s[bz], jnp.zeros((32, 256), BF16)
            got = jnp.dot(
                jnp.concatenate([window, window], axis=1),
                jnp.concatenate([high, high, none, low, low, none], axis=0),
                preferred_element_type=F32,
            )
            at = pl.ds(pl.multiple_of(8 * bz, 8), 8)
            for by in range(2):
                fz, fzt = fz_s[by, at, :], fzt_s[by, at, :]
                u = [got[8 * c : 8 * c + 8, 128 * by : 128 * by + 128] for c in range(4)]
                for c in range(3):
                    red_s[2 * c + by, at, :] = fz * u[c]
                red_s[6 + by, at, :] = fz * u[3] + fzt * u[2]
        return carry

    lax.fori_loop(0, 16, body, 0, unroll=16)

    for j in range(8):
        here, cx, cy, cz, by, pos_x, pos_y = coords(cell_ref, frac, j)
        sums = []
        for c in range(4):
            parts = [red_s[2 * c + by, pl.ds(64 * (j % 4) + s, 8, stride=8), :] for s in range(8)]
            while len(parts) > 1:
                parts = [parts[k] + parts[k + 1] for k in range(0, len(parts), 2)]
            sums.append(parts[0])
        live = live_s[here, :] > 0.5
        rate = sums[3] - pos_x * sums[0] - pos_y * sums[1] - (frac[2, here, :] - 0.5) * sums[2]
        stress_out[here, :] = stress[here, :] - jnp.where(live, (4.0 * 4.0 * DT) * rate, 0.0)
        for e in range(3):
            f = frac[e, here, :]
            frac_out[e, here, :] = jnp.where(live, f + DT * sums[e], f)
            vel_out[e, here, :] = jnp.where(live, sums[e], vel[e, here, :])


def nodes_kernel(
    cell_hbm,
    count_hbm,
    frac_hbm,
    vel_hbm,
    mass_hbm,
    stress_hbm,
    drag_hbm,
    cell_ref,
    live_s,
    frac_mid,
    vel_mid,
    stress_mid,
    ph_s,
    pl_s,
    fz_s,
    fzt_s,
    vt_s,
    count_ref,
    frac_in,
    vel_in,
    mass_ref,
    stress_in,
    drag_ref,
    rows_s,
    base_s,
    even_s,
    odd_s,
    red_s,
    grid_s,
    edge_s,
    left_s,
    right_s,
    cross_left_s,
    cross_right_s,
    other_s,
    load_sem,
    send_sem,
    recv_sem,
):
    n_space = lax.axis_size("space")
    me = lax.axis_index("space")
    phase = lax.axis_index("phase")
    right = lax.rem(me + 1, n_space)
    left = lax.rem(me + n_space - 1, n_space)
    to_left = (left, phase)
    to_right = (right, phase)
    to_other = (me, 1 - phase)
    to_cross_left = (left, 1 - phase)
    to_cross_right = (right, 1 - phase)

    has_left = me > 0
    has_right = me < n_space - 1
    run_left = lax.rem(me, RUN) == 0
    run_right = lax.rem(me, RUN) == RUN - 1
    cross_left = jnp.logical_and(has_left, run_left)
    cross_right = jnp.logical_and(has_right, run_right)
    barrier = pltpu.get_barrier_semaphore()

    def greet(target):
        pl.semaphore_signal(barrier, inc=1, device_id=target, device_id_type=MESH)

    greet(to_other)
    pl.when(has_left)(lambda: greet(to_left))
    pl.when(has_right)(lambda: greet(to_right))
    pl.when(cross_left)(lambda: greet(to_cross_left))
    pl.when(cross_right)(lambda: greet(to_cross_right))
    greeted = 1 + sum(flag.astype(jnp.int32) for flag in (has_left, has_right, cross_left, cross_right))

    loads = [
        pltpu.make_async_copy(src, dst, load_sem.at[k])
        for k, (src, dst) in enumerate(
            (
                (frac_hbm, frac_in),
                (cell_hbm, cell_ref),
                (count_hbm, count_ref),
                (vel_hbm, vel_in),
                (mass_hbm, mass_ref),
                (stress_hbm, stress_in),
                (drag_hbm, drag_ref),
            )
        )
    ]
    for load in loads:
        load.start()

    def remote(src, dst, sem, target):
        return pltpu.make_async_remote_copy(
            src_ref=src,
            dst_ref=dst,
            send_sem=send_sem.at[sem],
            recv_sem=recv_sem.at[sem],
            device_id=target,
            device_id_type=MESH,
        )

    sub8 = lax.broadcasted_iota(jnp.int32, (8, 128), 0)
    zero8 = jnp.zeros((8, 128), F32)
    for c in range(5):
        even_s[c, 128:136, :] = zero8
        odd_s[c, 0:8, :] = zero8
    for c in range(4):
        vt_s[c, 0:8, :] = zero8
        vt_s[c, 136:144, :] = zero8

    for load in loads:
        load.wait()

    diagonal = lax.broadcasted_iota(jnp.int32, (64, 64), 0) == lax.broadcasted_iota(jnp.int32, (64, 64), 1)
    counts = jnp.broadcast_to(count_ref[...].astype(F32), (64, 64))
    counts = jnp.sum(jnp.where(diagonal, counts, 0.0), axis=1, keepdims=True)
    slots = lax.broadcasted_iota(jnp.int32, (64, 128), 1).astype(F32)
    live_s[...] = jnp.where(slots < counts, 1.0, 0.0)

    def prepare(frac, vel, stress):
        for j in range(8):
            here, cx, cy, cz, by, pos_x, pos_y = coords(cell_ref, frac, j)
            wx = factors(frac[0, here, :])
            wy = factors(frac[1, here, :])
            wz = factors(frac[2, here, :])
            at = [cx == k for k in range(4)]
            for a in range(6):
                value = zero8
                for k in range(4):
                    if 0 <= a - k <= 2:
                        value = jnp.where(at[k], wx[a - k], value)
                rows_s[FX + a, here, :] = value
            for k in range(3):
                rows_s[WY + k, here, :] = wy[k]
                rows_s[WZ + k, here, :] = wz[k]
            base_s[0, here, :] = cy + (4 * by - 1)
            base_s[1, here, :] = (cz + 4 * (sub8 & 1) - 1) & 7
            live = live_s[here, :] > 0.5
            m = jnp.where(live, mass_ref[here, :], 0.0)
            s2 = jnp.where(live, stress[here, :], 0.0) * (4.0 * DT)
            rows_s[MASS, here, :] = m
            rows_s[S2, here, :] = s2
            rows_s[QX, here, :] = m * vel[0, here, :] - s2 * pos_x
            rows_s[QY, here, :] = m * vel[1, here, :] - s2 * pos_y
            rows_s[QZ, here, :] = m * vel[2, here, :] - s2 * (frac[2, here, :] - 0.5)

    def deposit(step):
        def body(i, carry):
            for par in range(2):
                bz = 2 * i + par
                plane = []
                column = []
                for by in range(2):
                    at = pl.ds(bz + 32 * by, 1)

                    def row(f):
                        return jnp.broadcast_to(rows_s[f, at, :], (8, 128))

                    t = sub8 - jnp.broadcast_to(base_s[0, at, :], (8, 128))
                    fy = jnp.where(t == 0, row(WY), jnp.where(t == 1, row(WY + 1), jnp.where(t == 2, row(WY + 2), 0.0)))
                    t = (sub8 - jnp.broadcast_to(base_s[1, at, :], (8, 128))) & 7
                    fz = jnp.where(t == 0, row(WZ), jnp.where(t == 1, row(WZ + 1), jnp.where(t == 2, row(WZ + 2), 0.0)))
                    tm1 = (t - 1).astype(F32)
                    s2 = row(S2)
                    plane.append(jnp.concatenate([row(FX + a) * fy for a in range(6)], axis=0))
                    column.append(
                        jnp.concatenate(
                            [
                                row(MASS) * fz,
                                row(QX) * fz,
                                row(QY) * fz,
                                (row(QZ) + s2 * tm1) * fz,
                                s2 * fz,
                            ],
                            axis=0,
                        )
                    )
                    here = pl.ds(pl.multiple_of(8 * bz, 8), 8)
                    fz_s[by, here, :] = fz
                    fzt_s[by, here, :] = fz * tm1
                plane_hi, plane_lo = split(jnp.concatenate(plane, axis=1))
                ph_s[bz] = plane_hi
                pl_s[bz] = plane_lo
                column_hi, column_lo = split(jnp.concatenate(column, axis=1))
                out = lax.dot_general(
                    jnp.concatenate([column_hi, column_lo], axis=0),
                    jnp.concatenate([plane_hi, plane_lo, jnp.zeros((32, 256), BF16)], axis=0),
                    (((1,), (1,)), ((), ())),
                    preferred_element_type=F32,
                )
                out = out[:40] + out[40:]
                for c in range(5):
                    if par == 0:
                        even_s[c, pl.ds(pl.multiple_of(8 * i, 8), 8), :] = out[8 * c : 8 * c + 8]
                    else:
                        odd_s[c, pl.ds(pl.multiple_of(8 * i + 8, 8), 8), :] = out[8 * c : 8 * c + 8]
            return carry

        lax.fori_loop(0, 16, body, 0, unroll=16)
        fields = []
        row7 = (lax.broadcasted_iota(jnp.int32, (128, 128), 0) & 7) == 7
        row0 = (lax.broadcasted_iota(jnp.int32, (128, 128), 0) & 7) == 0
        for c in range(5):
            total = jnp.where(row7, even_s[c, 8:136, :], even_s[c, 0:128, :]) + jnp.where(
                row0, odd_s[c, 0:128, :], odd_s[c, 8:136, :]
            )
            turned = total.T
            fields.append((turned[0:48] + turned[48:96]).reshape(6, 8, 128))
        y = sub8.astype(F32) - 3.5
        for a in range(6):
            grid_s[step, a, 0] = fields[0][a]
            grid_s[step, a, 1] = fields[1][a] + (a - 2.5) * fields[4][a]
            grid_s[step, a, 2] = fields[2][a] + y * fields[4][a]
            grid_s[step, a, 3] = fields[3][a]

    floor = lax.broadcasted_iota(jnp.int32, (8, 128), 1) == 0

    def velocity(mass, momentum):
        inverse = 1.0 / jnp.maximum(mass, 0.25)
        v = [momentum[e] * inverse for e in range(3)]
        v[2] = v[2] - DT
        v[2] = jnp.where(floor, jnp.maximum(v[2], 0.0), v[2])
        return v

    def turn(node_vel):
        y = sub8.astype(F32) - 3.5
        for c in range(4):
            if c < 3:
                values = [node_vel[a][c] for a in range(6)]
            else:
                values = [(a - 2.5) * node_vel[a][0] + y * node_vel[a][1] for a in range(6)]
            values = jnp.concatenate(values, axis=0)
            high = values.astype(BF16).astype(F32)
            turned = jnp.concatenate([high, values - high, jnp.zeros((32, 128), F32)], axis=0).T
            vt_s[c, 8:136, :] = turned

    def settled(a, c, mine, from_left, from_right, use_left, use_right):
        if a < 2:
            return mine[a, c] + jnp.where(use_left, from_left[a, c], 0.0)
        if a < 4:
            return mine[a, c]
        return mine[a, c] + jnp.where(use_right, from_right[a - 4, c], 0.0)

    started = []
    for step in range(2):
        state = (frac_in, vel_in, stress_in) if step == 0 else (frac_mid, vel_mid, stress_mid)
        prepare(*state)
        deposit(step)
        mine = grid_s.at[step]
        width = 5 if step == 0 else 4
        leftward = remote(mine.at[0:2, 0:width], right_s.at[step, :, 0:width], 2 * step, to_left)
        rightward = remote(mine.at[4:6, 0:width], left_s.at[step, :, 0:width], 2 * step + 1, to_right)
        started += [(has_left, leftward), (has_right, rightward)]
        if step == 0:
            for a in range(1, 5):
                mine[a, 4] = drag_ref[a - 1]
            mine[0, 4] = zero8
            mine[5, 4] = zero8
            pl.semaphore_wait(barrier, greeted)
        pl.when(has_left)(leftward.start)
        pl.when(has_right)(rightward.start)
        if step == 0:
            inner = remote(mine.at[2:4, 0:4], other_s.at[2:4], 4, to_other)
            inner.start()
            cross_leftward = remote(mine.at[0:2, 0:4], cross_right_s, 5, to_cross_left)
            cross_rightward = remote(mine.at[4:6, 0:4], cross_left_s, 6, to_cross_right)
            raw_left = remote(mine.at[0:2, 0:4], other_s.at[0:2], 7, to_other)
            raw_right = remote(mine.at[4:6, 0:4], other_s.at[4:6], 8, to_other)
            sum_left = remote(edge_s.at[0:2], other_s.at[0:2], 7, to_other)
            sum_right = remote(edge_s.at[2:4], other_s.at[4:6], 8, to_other)

            def send_raw(flag, run, cross, raw):
                pl.when(flag)(cross.start)
                pl.when(run)(raw.start)

            send_raw(cross_left, run_left, cross_leftward, raw_left)
            send_raw(cross_right, run_right, cross_rightward, raw_right)
            started += [(cross_left, cross_leftward), (cross_right, cross_rightward)]
            started += [(None, inner), (None, sum_left), (None, sum_right)]

            def send_sum_left():
                rightward.wait_recv()
                for a in range(2):
                    for c in range(4):
                        edge_s[a, c] = mine[a, c] + left_s[0, a, c]
                sum_left.start()

            def send_sum_right():
                leftward.wait_recv()
                for a in range(2):
                    for c in range(4):
                        edge_s[2 + a, c] = mine[4 + a, c] + right_s[0, a, c]
                sum_right.start()

            near_left = lax.rem(me, 2) == 1
            pl.when(near_left)(send_sum_left)
            pl.when(jnp.logical_not(run_right))(send_sum_right)
            pl.when(jnp.logical_not(jnp.logical_or(near_left, run_left)))(send_sum_left)
            pl.when(cross_left)(rightward.wait_recv)
            pl.when(cross_right)(leftward.wait_recv)
            inner.wait_recv()
            pl.when(cross_left)(cross_rightward.wait_recv)
            pl.when(cross_right)(cross_leftward.wait_recv)
            sum_left.wait_recv()
            sum_right.wait_recv()
        else:
            pl.when(has_left)(rightward.wait_recv)
            pl.when(has_right)(leftward.wait_recv)
        node_vel = []
        for a in range(6):
            full = [settled(a, c, mine, left_s.at[step], right_s.at[step], has_left, has_right) for c in range(4)]
            v = velocity(full[0], full[1:])
            if step == 0:
                other = [settled(a, c, other_s, cross_left_s, cross_right_s, cross_left, cross_right) for c in range(4)]
                other_vel = velocity(other[0], other[1:])
                coef = left_s[0, 0, 4] if a == 0 else right_s[0, 1, 4] if a == 5 else drag_ref[a - 1]
                slip = [other_vel[e] - v[e] for e in range(3)]
                rate = coef * jnp.sqrt(slip[0] * slip[0] + slip[1] * slip[1] + slip[2] * slip[2] + 0.25)
                gain = rate / (1.0 + rate) * (other[0] / (full[0] + other[0] + 0.25))
                v = [v[e] + gain * slip[e] for e in range(3)]
            if a == 0:
                v = [jnp.where(has_left, value, 0.0) for value in v]
            if a == 5:
                v = [jnp.where(has_right, value, 0.0) for value in v]
            node_vel.append(v)
        turn(node_vel)
        if step == 0:
            gather(
                vt_s, ph_s, pl_s, fz_s, fzt_s, red_s, cell_ref, live_s, state, (frac_mid, vel_mid, stress_mid)
            )
    for flag, copy in started:
        if flag is None:
            copy.wait_send()
        else:
            pl.when(flag)(copy.wait_send)


def particles_kernel(
    cell_ref,
    live_s,
    frac_mid,
    vel_mid,
    stress_mid,
    ph_s,
    pl_s,
    fz_s,
    fzt_s,
    vt_s,
    frac_hbm,
    vel_hbm,
    stress_hbm,
    frac_out,
    vel_out,
    stress_out,
    red_s,
    store_sem,
):
    gather(
        vt_s,
        ph_s,
        pl_s,
        fz_s,
        fzt_s,
        red_s,
        cell_ref,
        live_s,
        (frac_mid, vel_mid, stress_mid),
        (frac_out, vel_out, stress_out),
    )
    stores = [
        pltpu.make_async_copy(src, dst, store_sem.at[k])
        for k, (src, dst) in enumerate(((frac_out, frac_hbm), (vel_out, vel_hbm), (stress_out, stress_hbm)))
    ]
    for store in stores:
        store.start()
    for store in stores:
        store.wait()


def local(cell, count, frac, vel, mass, stress, drag):
    vmem = pl.BlockSpec(memory_space=pltpu.VMEM)
    anywhere = pl.BlockSpec(memory_space=pl.ANY)
    passed = [
        ((64, 128), jnp.int32),
        ((64, 128), F32),
        ((3, 64, 128), F32),
        ((3, 64, 128), F32),
        ((64, 128), F32),
        ((32, 48, 256), BF16),
        ((32, 48, 256), BF16),
        ((2, 256, 128), F32),
        ((2, 256, 128), F32),
        ((4, 144, 128), F32),
    ]
    state = pl.pallas_call(
        nodes_kernel,
        out_shape=[jax.ShapeDtypeStruct(shape, kind) for shape, kind in passed],
        in_specs=[anywhere] * 7,
        out_specs=[vmem] * len(passed),
        scratch_shapes=[
            pltpu.VMEM((1, 64), jnp.int32),
            pltpu.VMEM((3, 64, 128), F32),
            pltpu.VMEM((3, 64, 128), F32),
            pltpu.VMEM((64, 128), F32),
            pltpu.VMEM((64, 128), F32),
            pltpu.VMEM((4, 8, 128), F32),
            pltpu.VMEM((NROW, 64, 128), F32),
            pltpu.VMEM((2, 64, 128), jnp.int32),
            pltpu.VMEM((5, 136, 128), F32),
            pltpu.VMEM((5, 136, 128), F32),
            pltpu.VMEM((8, 256, 128), F32),
            pltpu.VMEM((2, 6, 5, 8, 128), F32),
            pltpu.VMEM((4, 4, 8, 128), F32),
            pltpu.VMEM((2, 2, 5, 8, 128), F32),
            pltpu.VMEM((2, 2, 5, 8, 128), F32),
            pltpu.VMEM((2, 4, 8, 128), F32),
            pltpu.VMEM((2, 4, 8, 128), F32),
            pltpu.VMEM((6, 4, 8, 128), F32),
            pltpu.SemaphoreType.DMA((7,)),
            pltpu.SemaphoreType.DMA((9,)),
            pltpu.SemaphoreType.DMA((9,)),
        ],
        compiler_params=pltpu.CompilerParams(
            collective_id=0, has_side_effects=True, vmem_limit_bytes=24 * 1024 * 1024
        ),
    )(*[pltpu.with_memory_space_constraint(x, pltpu.HBM) for x in (cell[0], count, frac[0], vel[0], mass[0], stress[0], drag)])
    frac_out, vel_out, stress_out = pl.pallas_call(
        particles_kernel,
        out_shape=[
            jax.ShapeDtypeStruct((3, 64, 128), F32),
            jax.ShapeDtypeStruct((3, 64, 128), F32),
            jax.ShapeDtypeStruct((64, 128), F32),
        ],
        in_specs=[vmem] * len(passed),
        out_specs=[anywhere] * 3,
        scratch_shapes=[
            pltpu.VMEM((3, 64, 128), F32),
            pltpu.VMEM((3, 64, 128), F32),
            pltpu.VMEM((64, 128), F32),
            pltpu.VMEM((8, 256, 128), F32),
            pltpu.SemaphoreType.DMA((3,)),
        ],
        compiler_params=pltpu.CompilerParams(vmem_limit_bytes=24 * 1024 * 1024),
    )(*state)
    return frac_out[None], vel_out[None], stress_out[None]


def solution(mesh):
    in_specs = (
        P("phase", "space", None),
        P("phase", "space"),
        P("phase", None, "space", None),
        P("phase", None, "space", None),
        P("phase", "space", None),
        P("phase", "space", None),
        P("space", None, None),
    )
    out_specs = (
        P("phase", None, "space", None),
        P("phase", None, "space", None),
        P("phase", "space", None),
    )
    return jax.shard_map(local, mesh=mesh, in_specs=in_specs, out_specs=out_specs, check_vma=False)
```

```python
import jax
import jax.numpy as jnp
from jax import lax
from jax.experimental import pallas as pl
from jax.experimental.pallas import tpu as pltpu
from jax.sharding import PartitionSpec as P

F32 = jnp.float32
BF16 = jnp.bfloat16
DT = 0.05
MESH = pl.DeviceIdType.MESH
RUN = 32

FX, MASS, QX, QY, QZ, S2 = 0, 6, 7, 8, 9, 10
NROW = 11


def split(value):
    high = value.astype(BF16)
    low = (value - high.astype(F32)).astype(BF16)
    return high, low


def factors(frac):
    r = frac - 0.5
    return 0.5 * (0.5 - r) * (0.5 - r), 0.75 - r * r, 0.5 * (0.5 + r) * (0.5 + r)


def coords(cell_ref, frac, j):
    here = pl.ds(8 * j, 8)
    cell = cell_ref[here, :]
    cx = cell >> 4
    cy = (cell >> 2) & 3
    cz = cell & 3
    by = j // 4
    pos_x = cx.astype(F32) + (frac[0, here, :] - 2.0)
    pos_y = (cy + 4 * by).astype(F32) + (frac[1, here, :] - 4.0)
    return here, cx, cy, cz, by, pos_x, pos_y


def gather(vt_s, ph_s, pl_s, fz_s, fzt_s, red_s, cell_ref, live_s, state, out):
    frac, vel, stress = state
    frac_out, vel_out, stress_out = out
    sub8 = lax.broadcasted_iota(jnp.int32, (8, 128), 0)

    def body(i, carry):
        for par in range(2):
            bz = 2 * i + par
            window = []
            for c in range(4):
                here = vt_s[c, pl.ds(pl.multiple_of(8 * i + 8, 8), 8), :]
                if par == 0:
                    beside = vt_s[c, pl.ds(pl.multiple_of(8 * i, 8), 8), :]
                    window.append(jnp.where(sub8 == 7, beside, here))
                else:
                    beside = vt_s[c, pl.ds(pl.multiple_of(8 * i + 16, 8), 8), :]
                    window.append(jnp.where(sub8 == 0, beside, here))
            window = jnp.concatenate(window, axis=0).astype(BF16)
            high, low, none = ph_s[bz], pl_s[bz], jnp.zeros((32, 256), BF16)
            got = jnp.dot(
                jnp.concatenate([window, window], axis=1),
                jnp.concatenate([high, high, none, low, low, none], axis=0),
                preferred_element_type=F32,
            )
            at = pl.ds(pl.multiple_of(8 * bz, 8), 8)
            for by in range(2):
                fz, fzt = fz_s[by, at, :], fzt_s[by, at, :]
                u = [got[8 * c : 8 * c + 8, 128 * by : 128 * by + 128] for c in range(4)]
                for c in range(3):
                    red_s[2 * c + by, at, :] = fz * u[c]
                red_s[6 + by, at, :] = fz * u[3] + fzt * u[2]
        return carry

    lax.fori_loop(0, 16, body, 0, unroll=16)

    for j in range(8):
        here, cx, cy, cz, by, pos_x, pos_y = coords(cell_ref, frac, j)
        sums = []
        for c in range(4):
            parts = [red_s[2 * c + by, pl.ds(64 * (j % 4) + s, 8, stride=8), :] for s in range(8)]
            while len(parts) > 1:
                parts = [parts[k] + parts[k + 1] for k in range(0, len(parts), 2)]
            sums.append(parts[0])
        live = live_s[here, :] > 0.5
        rate = sums[3] - pos_x * sums[0] - pos_y * sums[1] - (frac[2, here, :] - 0.5) * sums[2]
        stress_out[here, :] = stress[here, :] - jnp.where(live, (4.0 * 4.0 * DT) * rate, 0.0)
        for e in range(3):
            f = frac[e, here, :]
            frac_out[e, here, :] = jnp.where(live, f + DT * sums[e], f)
            vel_out[e, here, :] = jnp.where(live, sums[e], vel[e, here, :])


def nodes_kernel(
    cell_hbm,
    count_hbm,
    frac_hbm,
    vel_hbm,
    mass_hbm,
    stress_hbm,
    drag_hbm,
    cell_ref,
    live_s,
    frac_mid,
    vel_mid,
    stress_mid,
    ph_s,
    pl_s,
    fz_s,
    fzt_s,
    vt_s,
    count_ref,
    frac_in,
    vel_in,
    mass_ref,
    stress_in,
    drag_ref,
    rows_s,
    fy_s,
    even_s,
    odd_s,
    red_s,
    grid_s,
    edge_s,
    left_s,
    right_s,
    cross_left_s,
    cross_right_s,
    other_s,
    load_sem,
    send_sem,
    recv_sem,
):
    n_space = lax.axis_size("space")
    me = lax.axis_index("space")
    phase = lax.axis_index("phase")
    right = lax.rem(me + 1, n_space)
    left = lax.rem(me + n_space - 1, n_space)
    to_left = (left, phase)
    to_right = (right, phase)
    to_other = (me, 1 - phase)
    to_cross_left = (left, 1 - phase)
    to_cross_right = (right, 1 - phase)

    has_left = me > 0
    has_right = me < n_space - 1
    run_left = lax.rem(me, RUN) == 0
    run_right = lax.rem(me, RUN) == RUN - 1
    cross_left = jnp.logical_and(has_left, run_left)
    cross_right = jnp.logical_and(has_right, run_right)
    relay_left = jnp.logical_and(cross_left, phase == 0)
    relay_right = jnp.logical_and(cross_right, phase == 0)
    direct_left = jnp.logical_and(has_left, jnp.logical_not(jnp.logical_and(run_left, phase == 1)))
    direct_right = jnp.logical_and(has_right, jnp.logical_not(jnp.logical_and(run_right, phase == 1)))
    barrier = pltpu.get_barrier_semaphore()

    def greet(target):
        pl.semaphore_signal(barrier, inc=1, device_id=target, device_id_type=MESH)

    greet(to_other)
    pl.when(direct_left)(lambda: greet(to_left))
    pl.when(direct_right)(lambda: greet(to_right))
    pl.when(cross_left)(lambda: greet(to_cross_left))
    pl.when(cross_right)(lambda: greet(to_cross_right))
    greeted = 1 + sum(flag.astype(jnp.int32) for flag in (direct_left, direct_right, cross_left, cross_right))

    loads = [
        pltpu.make_async_copy(src, dst, load_sem.at[k])
        for k, (src, dst) in enumerate(
            (
                (frac_hbm, frac_in),
                (cell_hbm, cell_ref),
                (count_hbm, count_ref),
                (vel_hbm, vel_in),
                (mass_hbm, mass_ref),
                (stress_hbm, stress_in),
                (drag_hbm, drag_ref),
            )
        )
    ]
    for load in loads:
        load.start()

    def remote(src, dst, sem, target, arrival=None):
        return pltpu.make_async_remote_copy(
            src_ref=src,
            dst_ref=dst,
            send_sem=send_sem.at[sem],
            recv_sem=recv_sem.at[sem if arrival is None else arrival],
            device_id=target,
            device_id_type=MESH,
        )

    sub8 = lax.broadcasted_iota(jnp.int32, (8, 128), 0)
    zero8 = jnp.zeros((8, 128), F32)
    for c in range(5):
        even_s[c, 128:136, :] = zero8
        odd_s[c, 0:8, :] = zero8
    fy_s[...] = jnp.zeros((2, 256, 128), F32)
    for c in range(4):
        vt_s[c, 0:8, :] = zero8
        vt_s[c, 136:144, :] = zero8

    for load in loads:
        load.wait()

    diagonal = lax.broadcasted_iota(jnp.int32, (64, 64), 0) == lax.broadcasted_iota(jnp.int32, (64, 64), 1)
    counts = jnp.broadcast_to(count_ref[...].astype(F32), (64, 64))
    counts = jnp.sum(jnp.where(diagonal, counts, 0.0), axis=1, keepdims=True)
    slots = lax.broadcasted_iota(jnp.int32, (64, 128), 1).astype(F32)
    live_s[...] = jnp.where(slots < counts, 1.0, 0.0)

    def prepare(frac, vel, stress):
        for j in range(8):
            here, cx, cy, cz, by, pos_x, pos_y = coords(cell_ref, frac, j)
            wx = factors(frac[0, here, :])
            wy = factors(frac[1, here, :])
            wz = factors(frac[2, here, :])
            on_x = [cx == k for k in range(4)]
            on_y = [cy == k for k in range(4)]
            on_z = [cz == k for k in range(4)]

            def place(on, w, node):
                value = zero8
                for k in range(4):
                    if 0 <= node - k <= 2 and w[node - k] is not None:
                        value = jnp.where(on[k], w[node - k], value)
                return value

            for a in range(6):
                rows_s[FX + a, here, :] = place(on_x, wx, a)
            start = 64 * (j % 4)
            for node in range(6):
                y = 4 * by + node - 1
                if 0 <= y < 8:
                    fy_s[by, pl.ds(start + y, 8, stride=8), :] = place(on_y, wy, node)
            tz = (-wz[0], None, wz[2])
            for ref, w in ((fz_s, wz), (fzt_s, tz)):
                nodes = [place(on_z, w, node) for node in range(6)] + [zero8, zero8]
                for r in range(8):
                    value = jnp.where((sub8 & 1) == 0, nodes[(r + 1) % 8], nodes[(r + 5) % 8])
                    ref[by, pl.ds(start + r, 8, stride=8), :] = value
            live = live_s[here, :] > 0.5
            m = jnp.where(live, mass_ref[here, :], 0.0)
            s2 = jnp.where(live, stress[here, :], 0.0) * (4.0 * DT)
            rows_s[MASS, here, :] = m
            rows_s[S2, here, :] = s2
            rows_s[QX, here, :] = m * vel[0, here, :] - s2 * pos_x
            rows_s[QY, here, :] = m * vel[1, here, :] - s2 * pos_y
            rows_s[QZ, here, :] = m * vel[2, here, :] - s2 * (frac[2, here, :] - 0.5)

    def deposit(step):
        def body(i, carry):
            for par in range(2):
                bz = 2 * i + par
                plane = []
                column = []
                for by in range(2):
                    at = pl.ds(bz + 32 * by, 1)

                    def row(f):
                        return jnp.broadcast_to(rows_s[f, at, :], (8, 128))

                    here = pl.ds(pl.multiple_of(8 * bz, 8), 8)
                    fy = fy_s[by, here, :]
                    fz = fz_s[by, here, :]
                    s2 = row(S2)
                    plane.append(jnp.concatenate([row(FX + a) * fy for a in range(6)], axis=0))
                    column.append(
                        jnp.concatenate(
                            [
                                row(MASS) * fz,
                                row(QX) * fz,
                                row(QY) * fz,
                                row(QZ) * fz + s2 * fzt_s[by, here, :],
                                s2 * fz,
                            ],
                            axis=0,
                        )
                    )
                plane_hi, plane_lo = split(jnp.concatenate(plane, axis=1))
                ph_s[bz] = plane_hi
                pl_s[bz] = plane_lo
                column_hi, column_lo = split(jnp.concatenate(column, axis=1))
                out = lax.dot_general(
                    jnp.concatenate([column_hi, column_lo], axis=0),
                    jnp.concatenate([plane_hi, plane_lo, jnp.zeros((32, 256), BF16)], axis=0),
                    (((1,), (1,)), ((), ())),
                    preferred_element_type=F32,
                )
                out = out[:40] + out[40:]
                for c in range(5):
                    if par == 0:
                        even_s[c, pl.ds(pl.multiple_of(8 * i, 8), 8), :] = out[8 * c : 8 * c + 8]
                    else:
                        odd_s[c, pl.ds(pl.multiple_of(8 * i + 8, 8), 8), :] = out[8 * c : 8 * c + 8]
            return carry

        lax.fori_loop(0, 16, body, 0, unroll=16)
        fields = []
        row7 = (lax.broadcasted_iota(jnp.int32, (128, 128), 0) & 7) == 7
        row0 = (lax.broadcasted_iota(jnp.int32, (128, 128), 0) & 7) == 0
        for c in range(5):
            total = jnp.where(row7, even_s[c, 8:136, :], even_s[c, 0:128, :]) + jnp.where(
                row0, odd_s[c, 0:128, :], odd_s[c, 8:136, :]
            )
            turned = total.T
            fields.append((turned[0:48] + turned[48:96]).reshape(6, 8, 128))
        y = sub8.astype(F32) - 3.5
        for a in range(6):
            grid_s[step, a, 0] = fields[0][a]
            grid_s[step, a, 1] = fields[1][a] + (a - 2.5) * fields[4][a]
            grid_s[step, a, 2] = fields[2][a] + y * fields[4][a]
            grid_s[step, a, 3] = fields[3][a]

    floor = lax.broadcasted_iota(jnp.int32, (8, 128), 1) == 0

    def velocity(mass, momentum):
        inverse = 1.0 / jnp.maximum(mass, 0.25)
        v = [momentum[e] * inverse for e in range(3)]
        v[2] = v[2] - DT
        v[2] = jnp.where(floor, jnp.maximum(v[2], 0.0), v[2])
        return v

    def turn(node_vel):
        y = sub8.astype(F32) - 3.5
        for c in range(4):
            if c < 3:
                values = [node_vel[a][c] for a in range(6)]
            else:
                values = [(a - 2.5) * node_vel[a][0] + y * node_vel[a][1] for a in range(6)]
            values = jnp.concatenate(values, axis=0)
            high = values.astype(BF16).astype(F32)
            turned = jnp.concatenate([high, values - high, jnp.zeros((32, 128), F32)], axis=0).T
            vt_s[c, 8:136, :] = turned

    def settled(a, c, mine, from_left, from_right, use_left, use_right):
        if a < 2:
            return mine[a, c] + jnp.where(use_left, from_left[a, c], 0.0)
        if a < 4:
            return mine[a, c]
        return mine[a, c] + jnp.where(use_right, from_right[a - 4, c], 0.0)

    started = []

    def own(a, step):
        mine = grid_s.at[step]
        full = [settled(a, c, mine, left_s.at[step], right_s.at[step], has_left, has_right) for c in range(4)]
        return full[0], velocity(full[0], full[1:])

    for step in range(2):
        state = (frac_in, vel_in, stress_in) if step == 0 else (frac_mid, vel_mid, stress_mid)
        prepare(*state)
        deposit(step)
        mine = grid_s.at[step]
        width = 5 if step == 0 else 4
        leftward = remote(mine.at[0:2, 0:width], right_s.at[step, :, 0:width], 2 * step, to_left)
        rightward = remote(mine.at[4:6, 0:width], left_s.at[step, :, 0:width], 2 * step + 1, to_right)
        go_left, go_right = (direct_left, direct_right) if step == 0 else (has_left, has_right)
        started += [(go_left, leftward), (go_right, rightward)]
        if step == 0:
            for a in range(1, 5):
                mine[a, 4] = drag_ref[a - 1]
            mine[0, 4] = zero8
            mine[5, 4] = zero8
            pl.semaphore_wait(barrier, greeted)
        if step == 0:
            inner = remote(mine.at[2:4, 0:4], other_s.at[2:4], 4, to_other)
            inner.start()
        pl.when(go_left)(leftward.start)
        pl.when(go_right)(rightward.start)
        node = {a: own(a, step) for a in (2, 3)}
        if step == 0:
            cross_leftward = remote(mine.at[0:2], cross_right_s, 5, to_cross_left)
            cross_rightward = remote(mine.at[4:6], cross_left_s, 6, to_cross_right)
            raw_left = remote(mine.at[0:2, 0:4], other_s.at[0:2], 7, to_other)
            raw_right = remote(mine.at[4:6, 0:4], other_s.at[4:6], 8, to_other)
            sum_left = remote(edge_s.at[0:2], other_s.at[0:2], 7, to_other)
            sum_right = remote(edge_s.at[2:4], other_s.at[4:6], 8, to_other)

            def send_raw(flag, run, cross, raw):
                pl.when(flag)(cross.start)
                pl.when(run)(raw.start)

            send_raw(cross_left, run_left, cross_leftward, raw_left)
            send_raw(cross_right, run_right, cross_rightward, raw_right)
            started += [(cross_left, cross_leftward), (cross_right, cross_rightward)]
            started += [(None, inner), (None, sum_left), (None, sum_right)]

            def send_sum_left():
                rightward.wait_recv()
                for a in range(2):
                    for c in range(4):
                        edge_s[a, c] = mine[a, c] + left_s[0, a, c]
                sum_left.start()

            def send_sum_right():
                leftward.wait_recv()
                for a in range(2):
                    for c in range(4):
                        edge_s[2 + a, c] = mine[4 + a, c] + right_s[0, a, c]
                sum_right.start()

            near_left = lax.rem(me, 2) == 1
            pl.when(near_left)(send_sum_left)
            pl.when(jnp.logical_not(run_right))(send_sum_right)
            pl.when(jnp.logical_not(jnp.logical_or(near_left, run_left)))(send_sum_left)
            pass_left = remote(cross_left_s, left_s.at[0], 9, to_other, 1)
            pass_right = remote(cross_right_s, right_s.at[0], 10, to_other, 0)
            started += [(relay_left, pass_left), (relay_right, pass_right)]

            def pass_on(cross, onward):
                cross.wait_recv()
                onward.start()

            pl.when(relay_left)(lambda: pass_on(cross_rightward, pass_left))
            pl.when(relay_right)(lambda: pass_on(cross_leftward, pass_right))
            pl.when(cross_left)(rightward.wait_recv)
            pl.when(cross_right)(leftward.wait_recv)
            for a in (0, 1, 4, 5):
                node[a] = own(a, step)
            inner.wait_recv()
            pl.when(jnp.logical_and(cross_left, phase == 1))(cross_rightward.wait_recv)
            pl.when(jnp.logical_and(cross_right, phase == 1))(cross_leftward.wait_recv)
            sum_left.wait_recv()
            sum_right.wait_recv()
        else:
            pl.when(has_left)(rightward.wait_recv)
            pl.when(has_right)(leftward.wait_recv)
            for a in (0, 1, 4, 5):
                node[a] = own(a, step)
        node_vel = []
        for a in range(6):
            mass, v = node[a]
            if step == 0:
                other = [settled(a, c, other_s, cross_left_s, cross_right_s, cross_left, cross_right) for c in range(4)]
                other_vel = velocity(other[0], other[1:])
                coef = left_s[0, 0, 4] if a == 0 else right_s[0, 1, 4] if a == 5 else drag_ref[a - 1]
                slip = [other_vel[e] - v[e] for e in range(3)]
                rate = coef * jnp.sqrt(slip[0] * slip[0] + slip[1] * slip[1] + slip[2] * slip[2] + 0.25)
                gain = rate / (1.0 + rate) * (other[0] / (mass + other[0] + 0.25))
                v = [v[e] + gain * slip[e] for e in range(3)]
            if a == 0:
                v = [jnp.where(has_left, value, 0.0) for value in v]
            if a == 5:
                v = [jnp.where(has_right, value, 0.0) for value in v]
            node_vel.append(v)
        turn(node_vel)
        if step == 0:
            gather(
                vt_s, ph_s, pl_s, fz_s, fzt_s, red_s, cell_ref, live_s, state, (frac_mid, vel_mid, stress_mid)
            )
    for flag, copy in started:
        if flag is None:
            copy.wait_send()
        else:
            pl.when(flag)(copy.wait_send)


def particles_kernel(
    cell_ref,
    live_s,
    frac_mid,
    vel_mid,
    stress_mid,
    ph_s,
    pl_s,
    fz_s,
    fzt_s,
    vt_s,
    frac_hbm,
    vel_hbm,
    stress_hbm,
    frac_out,
    vel_out,
    stress_out,
    red_s,
    store_sem,
):
    gather(
        vt_s,
        ph_s,
        pl_s,
        fz_s,
        fzt_s,
        red_s,
        cell_ref,
        live_s,
        (frac_mid, vel_mid, stress_mid),
        (frac_out, vel_out, stress_out),
    )
    stores = [
        pltpu.make_async_copy(src, dst, store_sem.at[k])
        for k, (src, dst) in enumerate(((frac_out, frac_hbm), (vel_out, vel_hbm), (stress_out, stress_hbm)))
    ]
    for store in stores:
        store.start()
    for store in stores:
        store.wait()


def local(cell, count, frac, vel, mass, stress, drag):
    vmem = pl.BlockSpec(memory_space=pltpu.VMEM)
    anywhere = pl.BlockSpec(memory_space=pl.ANY)
    passed = [
        ((64, 128), jnp.int32),
        ((64, 128), F32),
        ((3, 64, 128), F32),
        ((3, 64, 128), F32),
        ((64, 128), F32),
        ((32, 48, 256), BF16),
        ((32, 48, 256), BF16),
        ((2, 256, 128), F32),
        ((2, 256, 128), F32),
        ((4, 144, 128), F32),
    ]
    state = pl.pallas_call(
        nodes_kernel,
        out_shape=[jax.ShapeDtypeStruct(shape, kind) for shape, kind in passed],
        in_specs=[anywhere] * 7,
        out_specs=[vmem] * len(passed),
        scratch_shapes=[
            pltpu.VMEM((1, 64), jnp.int32),
            pltpu.VMEM((3, 64, 128), F32),
            pltpu.VMEM((3, 64, 128), F32),
            pltpu.VMEM((64, 128), F32),
            pltpu.VMEM((64, 128), F32),
            pltpu.VMEM((4, 8, 128), F32),
            pltpu.VMEM((NROW, 64, 128), F32),
            pltpu.VMEM((2, 256, 128), F32),
            pltpu.VMEM((5, 136, 128), F32),
            pltpu.VMEM((5, 136, 128), F32),
            pltpu.VMEM((8, 256, 128), F32),
            pltpu.VMEM((2, 6, 5, 8, 128), F32),
            pltpu.VMEM((4, 4, 8, 128), F32),
            pltpu.VMEM((2, 2, 5, 8, 128), F32),
            pltpu.VMEM((2, 2, 5, 8, 128), F32),
            pltpu.VMEM((2, 5, 8, 128), F32),
            pltpu.VMEM((2, 5, 8, 128), F32),
            pltpu.VMEM((6, 4, 8, 128), F32),
            pltpu.SemaphoreType.DMA((7,)),
            pltpu.SemaphoreType.DMA((11,)),
            pltpu.SemaphoreType.DMA((9,)),
        ],
        compiler_params=pltpu.CompilerParams(
            collective_id=0, has_side_effects=True, vmem_limit_bytes=24 * 1024 * 1024
        ),
    )(*[pltpu.with_memory_space_constraint(x, pltpu.HBM) for x in (cell[0], count, frac[0], vel[0], mass[0], stress[0], drag)])
    frac_out, vel_out, stress_out = pl.pallas_call(
        particles_kernel,
        out_shape=[
            jax.ShapeDtypeStruct((3, 64, 128), F32),
            jax.ShapeDtypeStruct((3, 64, 128), F32),
            jax.ShapeDtypeStruct((64, 128), F32),
        ],
        in_specs=[vmem] * len(passed),
        out_specs=[anywhere] * 3,
        scratch_shapes=[
            pltpu.VMEM((3, 64, 128), F32),
            pltpu.VMEM((3, 64, 128), F32),
            pltpu.VMEM((64, 128), F32),
            pltpu.VMEM((8, 256, 128), F32),
            pltpu.SemaphoreType.DMA((3,)),
        ],
        compiler_params=pltpu.CompilerParams(vmem_limit_bytes=24 * 1024 * 1024),
    )(*state)
    return frac_out[None], vel_out[None], stress_out[None]


def solution(mesh):
    in_specs = (
        P("phase", "space", None),
        P("phase", "space"),
        P("phase", None, "space", None),
        P("phase", None, "space", None),
        P("phase", "space", None),
        P("phase", "space", None),
        P("space", None, None),
    )
    out_specs = (
        P("phase", None, "space", None),
        P("phase", None, "space", None),
        P("phase", "space", None),
    )
    return jax.shard_map(local, mesh=mesh, in_specs=in_specs, out_specs=out_specs, check_vma=False)
```

```python
import jax
import jax.numpy as jnp
from jax import lax
from jax.experimental import pallas as pl
from jax.experimental.pallas import tpu as pltpu
from jax.sharding import PartitionSpec as P

F32 = jnp.float32
BF16 = jnp.bfloat16
DT = 0.05
MESH = pl.DeviceIdType.MESH
RUN = 32
ROW = 8

FX, MASS, QX, QY, QZ, S2 = 0, 6, 7, 8, 9, 10
NROW = 11


def split(value):
    high = value.astype(BF16)
    low = (value - high.astype(F32)).astype(BF16)
    return high, low


def factors(frac):
    r = frac - 0.5
    return 0.5 * (0.5 - r) * (0.5 - r), 0.75 - r * r, 0.5 * (0.5 + r) * (0.5 + r)


def coords(cell_ref, frac, j):
    here = pl.ds(8 * j, 8)
    cell = cell_ref[here, :]
    cx = cell >> 4
    cy = (cell >> 2) & 3
    cz = cell & 3
    by = j // 4
    pos_x = cx.astype(F32) + (frac[0, here, :] - 2.0)
    pos_y = (cy + 4 * by).astype(F32) + (frac[1, here, :] - 4.0)
    return here, cx, cy, cz, by, pos_x, pos_y


def gather(vt_s, ph_s, pl_s, fz_s, fzt_s, red_s, cell_ref, live_s, state, out):
    frac, vel, stress = state
    frac_out, vel_out, stress_out = out
    sub8 = lax.broadcasted_iota(jnp.int32, (8, 128), 0)

    def body(i):
        for par in range(2):
            bz = 2 * i + par
            window = []
            for c in range(4):
                here = vt_s[c, pl.ds(pl.multiple_of(8 * i + 8, 8), 8), :]
                if par == 0:
                    beside = vt_s[c, pl.ds(pl.multiple_of(8 * i, 8), 8), :]
                    window.append(jnp.where(sub8 == 7, beside, here))
                else:
                    beside = vt_s[c, pl.ds(pl.multiple_of(8 * i + 16, 8), 8), :]
                    window.append(jnp.where(sub8 == 0, beside, here))
            window = jnp.concatenate(window, axis=0).astype(BF16)
            high, low, none = ph_s[bz], pl_s[bz], jnp.zeros((32, 256), BF16)
            got = jnp.dot(
                jnp.concatenate([window, window], axis=1),
                jnp.concatenate([high, high, none, low, low, none], axis=0),
                preferred_element_type=F32,
            )
            at = pl.ds(pl.multiple_of(8 * bz, 8), 8)
            for by in range(2):
                fz, fzt = fz_s[by, at, :], fzt_s[by, at, :]
                u = [got[8 * c : 8 * c + 8, 128 * by : 128 * by + 128] for c in range(4)]
                for c in range(3):
                    red_s[2 * c + by, at, :] = fz * u[c]
                red_s[6 + by, at, :] = fz * u[3] + fzt * u[2]

    def finish(j):
        here, cx, cy, cz, by, pos_x, pos_y = coords(cell_ref, frac, j)
        sums = []
        for c in range(4):
            parts = [red_s[2 * c + by, pl.ds(64 * (j % 4) + s, 8, stride=8), :] for s in range(8)]
            while len(parts) > 1:
                parts = [parts[k] + parts[k + 1] for k in range(0, len(parts), 2)]
            sums.append(parts[0])
        live = live_s[here, :] > 0.5
        rate = sums[3] - pos_x * sums[0] - pos_y * sums[1] - (frac[2, here, :] - 0.5) * sums[2]
        stress_out[here, :] = stress[here, :] - jnp.where(live, (4.0 * 4.0 * DT) * rate, 0.0)
        for e in range(3):
            f = frac[e, here, :]
            frac_out[e, here, :] = jnp.where(live, f + DT * sums[e], f)
            vel_out[e, here, :] = jnp.where(live, sums[e], vel[e, here, :])

    for chunk in range(4):
        for i in range(4 * chunk, 4 * chunk + 4):
            body(i)
        finish(chunk)
        finish(chunk + 4)


def nodes_kernel(
    cell_hbm,
    count_hbm,
    frac_hbm,
    vel_hbm,
    mass_hbm,
    stress_hbm,
    drag_hbm,
    cell_ref,
    live_s,
    frac_mid,
    vel_mid,
    stress_mid,
    ph_s,
    pl_s,
    fz_s,
    fzt_s,
    vt_s,
    count_ref,
    frac_in,
    vel_in,
    mass_ref,
    stress_in,
    drag_ref,
    rows_s,
    fy_s,
    even_s,
    odd_s,
    red_s,
    grid_s,
    edge_s,
    left_s,
    right_s,
    cross_left_s,
    cross_right_s,
    other_s,
    load_sem,
    send_sem,
    recv_sem,
    open_sem,
):
    n_space = lax.axis_size("space")
    me = lax.axis_index("space")
    phase = lax.axis_index("phase")
    right = lax.rem(me + 1, n_space)
    left = lax.rem(me + n_space - 1, n_space)
    to_left = (left, phase)
    to_right = (right, phase)
    to_other = (me, 1 - phase)
    to_cross_left = (left, 1 - phase)
    to_cross_right = (right, 1 - phase)

    has_left = me > 0
    has_right = me < n_space - 1
    run_left = lax.rem(me, RUN) == 0
    run_right = lax.rem(me, RUN) == RUN - 1
    cross_left = jnp.logical_and(has_left, run_left)
    cross_right = jnp.logical_and(has_right, run_right)
    relay_left = jnp.logical_and(cross_left, phase == 0)
    relay_right = jnp.logical_and(cross_right, phase == 0)
    direct_left = jnp.logical_and(has_left, jnp.logical_not(jnp.logical_and(run_left, phase == 1)))
    direct_right = jnp.logical_and(has_right, jnp.logical_not(jnp.logical_and(run_right, phase == 1)))
    row_left = jnp.logical_and(lax.rem(me, ROW) == 0, jnp.logical_not(run_left))
    row_right = jnp.logical_and(lax.rem(me, ROW) == ROW - 1, jnp.logical_not(run_right))
    raw_out_left = jnp.logical_or(run_left, jnp.logical_and(row_left, phase == 1))
    raw_out_right = jnp.logical_or(run_right, jnp.logical_and(row_right, phase == 1))
    out_left = jnp.logical_and(has_left, raw_out_left)
    out_right = jnp.logical_and(has_right, raw_out_right)
    in_left = jnp.logical_or(cross_left, jnp.logical_and(row_left, phase == 0))
    in_right = jnp.logical_or(cross_right, jnp.logical_and(row_right, phase == 0))
    barrier = pltpu.get_barrier_semaphore()

    def greet(target, sem=barrier):
        pl.semaphore_signal(sem, inc=1, device_id=target, device_id_type=MESH)

    def greet_across():
        greet(to_other)
        pl.when(in_left)(lambda: greet(to_cross_left))
        pl.when(in_right)(lambda: greet(to_cross_right))

    def answer_across():
        greet(to_other, open_sem)
        pl.when(cross_left)(lambda: greet(to_cross_left, open_sem))
        pl.when(cross_right)(lambda: greet(to_cross_right, open_sem))

    def count(*flags):
        return sum(flag.astype(jnp.int32) for flag in flags)

    pl.when(direct_left)(lambda: greet(to_left))
    pl.when(direct_right)(lambda: greet(to_right))
    pl.when(phase == 0)(greet_across)
    greeted = count(direct_left, direct_right) + phase * (1 + count(out_left, out_right))
    answered = 1 + count(cross_left, cross_right)

    loads = [
        pltpu.make_async_copy(src, dst, load_sem.at[k])
        for k, (src, dst) in enumerate(
            (
                (frac_hbm, frac_in),
                (cell_hbm, cell_ref),
                (count_hbm, count_ref),
                (vel_hbm, vel_in),
                (mass_hbm, mass_ref),
                (stress_hbm, stress_in),
                (drag_hbm, drag_ref),
            )
        )
    ]
    for load in loads:
        load.start()

    def remote(src, dst, sem, target, arrival=None):
        return pltpu.make_async_remote_copy(
            src_ref=src,
            dst_ref=dst,
            send_sem=send_sem.at[sem],
            recv_sem=recv_sem.at[sem if arrival is None else arrival],
            device_id=target,
            device_id_type=MESH,
        )

    sub8 = lax.broadcasted_iota(jnp.int32, (8, 128), 0)
    zero8 = jnp.zeros((8, 128), F32)
    for c in range(5):
        even_s[c, 128:136, :] = zero8
        odd_s[c, 0:8, :] = zero8
    fy_s[...] = jnp.zeros((2, 256, 128), F32)
    for c in range(4):
        vt_s[c, 0:8, :] = zero8
        vt_s[c, 136:144, :] = zero8

    for load in loads:
        load.wait()

    diagonal = lax.broadcasted_iota(jnp.int32, (64, 64), 0) == lax.broadcasted_iota(jnp.int32, (64, 64), 1)
    counts = jnp.broadcast_to(count_ref[...].astype(F32), (64, 64))
    counts = jnp.sum(jnp.where(diagonal, counts, 0.0), axis=1, keepdims=True)
    slots = lax.broadcasted_iota(jnp.int32, (64, 128), 1).astype(F32)
    live_s[...] = jnp.where(slots < counts, 1.0, 0.0)

    def prepare(chunk, frac, vel, stress):
        for j in (chunk, chunk + 4):
            here, cx, cy, cz, by, pos_x, pos_y = coords(cell_ref, frac, j)
            wx = factors(frac[0, here, :])
            wy = factors(frac[1, here, :])
            wz = factors(frac[2, here, :])
            on_x = [cx == k for k in range(4)]
            on_y = [cy == k for k in range(4)]
            on_z = [cz == k for k in range(4)]

            def place(on, w, node):
                value = zero8
                for k in range(4):
                    if 0 <= node - k <= 2 and w[node - k] is not None:
                        value = jnp.where(on[k], w[node - k], value)
                return value

            for a in range(6):
                rows_s[FX + a, here, :] = place(on_x, wx, a)
            start = 64 * (j % 4)
            for node in range(6):
                y = 4 * by + node - 1
                if 0 <= y < 8:
                    fy_s[by, pl.ds(start + y, 8, stride=8), :] = place(on_y, wy, node)
            tz = (-wz[0], None, wz[2])
            for ref, w in ((fz_s, wz), (fzt_s, tz)):
                nodes = [place(on_z, w, node) for node in range(6)] + [zero8, zero8]
                for r in range(8):
                    value = jnp.where((sub8 & 1) == 0, nodes[(r + 1) % 8], nodes[(r + 5) % 8])
                    ref[by, pl.ds(start + r, 8, stride=8), :] = value
            live = live_s[here, :] > 0.5
            m = jnp.where(live, mass_ref[here, :], 0.0)
            s2 = jnp.where(live, stress[here, :], 0.0) * (4.0 * DT)
            rows_s[MASS, here, :] = m
            rows_s[S2, here, :] = s2
            rows_s[QX, here, :] = m * vel[0, here, :] - s2 * pos_x
            rows_s[QY, here, :] = m * vel[1, here, :] - s2 * pos_y
            rows_s[QZ, here, :] = m * vel[2, here, :] - s2 * (frac[2, here, :] - 0.5)

    def deposit(step, state):
        def body(i):
            for par in range(2):
                bz = 2 * i + par
                plane = []
                column = []
                for by in range(2):
                    at = pl.ds(bz + 32 * by, 1)

                    def row(f):
                        return jnp.broadcast_to(rows_s[f, at, :], (8, 128))

                    here = pl.ds(pl.multiple_of(8 * bz, 8), 8)
                    fy = fy_s[by, here, :]
                    fz = fz_s[by, here, :]
                    s2 = row(S2)
                    plane.append(jnp.concatenate([row(FX + a) * fy for a in range(6)], axis=0))
                    column.append(
                        jnp.concatenate(
                            [
                                row(MASS) * fz,
                                row(QX) * fz,
                                row(QY) * fz,
                                row(QZ) * fz + s2 * fzt_s[by, here, :],
                                s2 * fz,
                            ],
                            axis=0,
                        )
                    )
                plane_hi, plane_lo = split(jnp.concatenate(plane, axis=1))
                ph_s[bz] = plane_hi
                pl_s[bz] = plane_lo
                column_hi, column_lo = split(jnp.concatenate(column, axis=1))
                out = lax.dot_general(
                    jnp.concatenate([column_hi, column_lo], axis=0),
                    jnp.concatenate([plane_hi, plane_lo, jnp.zeros((32, 256), BF16)], axis=0),
                    (((1,), (1,)), ((), ())),
                    preferred_element_type=F32,
                )
                out = out[:40] + out[40:]
                for c in range(5):
                    if par == 0:
                        even_s[c, pl.ds(pl.multiple_of(8 * i, 8), 8), :] = out[8 * c : 8 * c + 8]
                    else:
                        odd_s[c, pl.ds(pl.multiple_of(8 * i + 8, 8), 8), :] = out[8 * c : 8 * c + 8]

        for chunk in range(4):
            prepare(chunk, *state)
            for i in range(4 * chunk, 4 * chunk + 4):
                body(i)
        fields = []
        row7 = (lax.broadcasted_iota(jnp.int32, (128, 128), 0) & 7) == 7
        row0 = (lax.broadcasted_iota(jnp.int32, (128, 128), 0) & 7) == 0
        for c in range(5):
            total = jnp.where(row7, even_s[c, 8:136, :], even_s[c, 0:128, :]) + jnp.where(
                row0, odd_s[c, 0:128, :], odd_s[c, 8:136, :]
            )
            turned = total.T
            fields.append((turned[0:48] + turned[48:96]).reshape(6, 8, 128))
        y = sub8.astype(F32) - 3.5
        for a in range(6):
            grid_s[step, a, 0] = fields[0][a]
            grid_s[step, a, 1] = fields[1][a] + (a - 2.5) * fields[4][a]
            grid_s[step, a, 2] = fields[2][a] + y * fields[4][a]
            grid_s[step, a, 3] = fields[3][a]

    floor = lax.broadcasted_iota(jnp.int32, (8, 128), 1) == 0

    def velocity(mass, momentum):
        inverse = 1.0 / jnp.maximum(mass, 0.25)
        v = [momentum[e] * inverse for e in range(3)]
        v[2] = v[2] - DT
        v[2] = jnp.where(floor, jnp.maximum(v[2], 0.0), v[2])
        return v

    def turn(node_vel):
        y = sub8.astype(F32) - 3.5
        for c in range(4):
            if c < 3:
                values = [node_vel[a][c] for a in range(6)]
            else:
                values = [(a - 2.5) * node_vel[a][0] + y * node_vel[a][1] for a in range(6)]
            values = jnp.concatenate(values, axis=0)
            high = values.astype(BF16).astype(F32)
            turned = jnp.concatenate([high, values - high, jnp.zeros((32, 128), F32)], axis=0).T
            vt_s[c, 8:136, :] = turned

    def settled(a, c, mine, from_left, from_right, use_left, use_right):
        if a < 2:
            return mine[a, c] + jnp.where(use_left, from_left[a, c], 0.0)
        if a < 4:
            return mine[a, c]
        return mine[a, c] + jnp.where(use_right, from_right[a - 4, c], 0.0)

    started = []

    def own(a, step):
        mine = grid_s.at[step]
        full = [settled(a, c, mine, left_s.at[step], right_s.at[step], has_left, has_right) for c in range(4)]
        return full[0], velocity(full[0], full[1:])

    for step in range(2):
        state = (frac_in, vel_in, stress_in) if step == 0 else (frac_mid, vel_mid, stress_mid)
        deposit(step, state)
        mine = grid_s.at[step]
        width = 5 if step == 0 else 4
        leftward = remote(mine.at[0:2, 0:width], right_s.at[step, :, 0:width], 2 * step, to_left)
        rightward = remote(mine.at[4:6, 0:width], left_s.at[step, :, 0:width], 2 * step + 1, to_right)
        go_left, go_right = (direct_left, direct_right) if step == 0 else (has_left, has_right)
        started += [(go_left, leftward), (go_right, rightward)]
        if step == 0:
            for a in range(1, 5):
                mine[a, 4] = drag_ref[a - 1]
            mine[0, 4] = zero8
            mine[5, 4] = zero8
            pl.semaphore_wait(barrier, greeted)
            pl.when(phase == 1)(answer_across)
        if step == 0:
            inner = remote(mine.at[2:4, 0:4], other_s.at[2:4], 4, to_other)
            pl.when(phase == 1)(inner.start)
        pl.when(go_left)(leftward.start)
        pl.when(go_right)(rightward.start)
        node = {a: own(a, step) for a in (2, 3)}
        if step == 0:
            cross_leftward = remote(mine.at[0:2], cross_right_s, 5, to_cross_left)
            cross_rightward = remote(mine.at[4:6], cross_left_s, 6, to_cross_right)
            raw_left = remote(mine.at[0:2, 0:4], other_s.at[0:2], 7, to_other)
            raw_right = remote(mine.at[4:6, 0:4], other_s.at[4:6], 8, to_other)
            sum_left = remote(edge_s.at[0:2], other_s.at[0:2], 7, to_other)
            sum_right = remote(edge_s.at[2:4], other_s.at[4:6], 8, to_other)

            def begin_across():
                pl.semaphore_wait(open_sem, answered)
                inner.start()

            pl.when(phase == 0)(begin_across)

            def send_raw(flag, run, cross, raw):
                pl.when(flag)(cross.start)
                pl.when(run)(raw.start)

            send_raw(out_left, raw_out_left, cross_leftward, raw_left)
            send_raw(out_right, raw_out_right, cross_rightward, raw_right)
            started += [(out_left, cross_leftward), (out_right, cross_rightward)]
            started += [(None, inner), (None, sum_left), (None, sum_right)]

            def send_sum_left():
                rightward.wait_recv()
                for a in range(2):
                    for c in range(4):
                        edge_s[a, c] = mine[a, c] + left_s[0, a, c]
                sum_left.start()

            def send_sum_right():
                leftward.wait_recv()
                for a in range(2):
                    for c in range(4):
                        edge_s[2 + a, c] = mine[4 + a, c] + right_s[0, a, c]
                sum_right.start()

            near_left = lax.rem(me, 2) == 1
            pl.when(near_left)(send_sum_left)
            pl.when(jnp.logical_not(raw_out_right))(send_sum_right)
            pl.when(jnp.logical_not(jnp.logical_or(near_left, raw_out_left)))(send_sum_left)
            pass_left = remote(cross_left_s, left_s.at[0], 9, to_other, 1)
            pass_right = remote(cross_right_s, right_s.at[0], 10, to_other, 0)
            started += [(relay_left, pass_left), (relay_right, pass_right)]

            def pass_on(cross, onward):
                cross.wait_recv()
                onward.start()

            pl.when(relay_left)(lambda: pass_on(cross_rightward, pass_left))
            pl.when(relay_right)(lambda: pass_on(cross_leftward, pass_right))
            pl.when(out_left)(rightward.wait_recv)
            pl.when(out_right)(leftward.wait_recv)
            for a in (0, 1, 4, 5):
                node[a] = own(a, step)
            inner.wait_recv()
            pl.when(jnp.logical_and(in_left, jnp.logical_not(relay_left)))(cross_rightward.wait_recv)
            pl.when(jnp.logical_and(in_right, jnp.logical_not(relay_right)))(cross_leftward.wait_recv)
            sum_left.wait_recv()
            sum_right.wait_recv()
        else:
            pl.when(has_left)(rightward.wait_recv)
            pl.when(has_right)(leftward.wait_recv)
            for a in (0, 1, 4, 5):
                node[a] = own(a, step)
        node_vel = []
        for a in range(6):
            mass, v = node[a]
            if step == 0:
                other = [settled(a, c, other_s, cross_left_s, cross_right_s, in_left, in_right) for c in range(4)]
                other_vel = velocity(other[0], other[1:])
                coef = left_s[0, 0, 4] if a == 0 else right_s[0, 1, 4] if a == 5 else drag_ref[a - 1]
                slip = [other_vel[e] - v[e] for e in range(3)]
                rate = coef * jnp.sqrt(slip[0] * slip[0] + slip[1] * slip[1] + slip[2] * slip[2] + 0.25)
                gain = rate / (1.0 + rate) * (other[0] / (mass + other[0] + 0.25))
                v = [v[e] + gain * slip[e] for e in range(3)]
            if a == 0:
                v = [jnp.where(has_left, value, 0.0) for value in v]
            if a == 5:
                v = [jnp.where(has_right, value, 0.0) for value in v]
            node_vel.append(v)
        turn(node_vel)
        if step == 0:
            gather(
                vt_s, ph_s, pl_s, fz_s, fzt_s, red_s, cell_ref, live_s, state, (frac_mid, vel_mid, stress_mid)
            )
    for flag, copy in started:
        if flag is None:
            copy.wait_send()
        else:
            pl.when(flag)(copy.wait_send)


def particles_kernel(
    cell_ref,
    live_s,
    frac_mid,
    vel_mid,
    stress_mid,
    ph_s,
    pl_s,
    fz_s,
    fzt_s,
    vt_s,
    frac_hbm,
    vel_hbm,
    stress_hbm,
    frac_out,
    vel_out,
    stress_out,
    red_s,
    store_sem,
):
    gather(
        vt_s,
        ph_s,
        pl_s,
        fz_s,
        fzt_s,
        red_s,
        cell_ref,
        live_s,
        (frac_mid, vel_mid, stress_mid),
        (frac_out, vel_out, stress_out),
    )
    stores = [
        pltpu.make_async_copy(src, dst, store_sem.at[k])
        for k, (src, dst) in enumerate(((frac_out, frac_hbm), (vel_out, vel_hbm), (stress_out, stress_hbm)))
    ]
    for store in stores:
        store.start()
    for store in stores:
        store.wait()


def local(cell, count, frac, vel, mass, stress, drag):
    vmem = pl.BlockSpec(memory_space=pltpu.VMEM)
    anywhere = pl.BlockSpec(memory_space=pl.ANY)
    passed = [
        ((64, 128), jnp.int32),
        ((64, 128), F32),
        ((3, 64, 128), F32),
        ((3, 64, 128), F32),
        ((64, 128), F32),
        ((32, 48, 256), BF16),
        ((32, 48, 256), BF16),
        ((2, 256, 128), F32),
        ((2, 256, 128), F32),
        ((4, 144, 128), F32),
    ]
    state = pl.pallas_call(
        nodes_kernel,
        out_shape=[jax.ShapeDtypeStruct(shape, kind) for shape, kind in passed],
        in_specs=[anywhere] * 7,
        out_specs=[vmem] * len(passed),
        scratch_shapes=[
            pltpu.VMEM((1, 64), jnp.int32),
            pltpu.VMEM((3, 64, 128), F32),
            pltpu.VMEM((3, 64, 128), F32),
            pltpu.VMEM((64, 128), F32),
            pltpu.VMEM((64, 128), F32),
            pltpu.VMEM((4, 8, 128), F32),
            pltpu.VMEM((NROW, 64, 128), F32),
            pltpu.VMEM((2, 256, 128), F32),
            pltpu.VMEM((5, 136, 128), F32),
            pltpu.VMEM((5, 136, 128), F32),
            pltpu.VMEM((8, 256, 128), F32),
            pltpu.VMEM((2, 6, 5, 8, 128), F32),
            pltpu.VMEM((4, 4, 8, 128), F32),
            pltpu.VMEM((2, 2, 5, 8, 128), F32),
            pltpu.VMEM((2, 2, 5, 8, 128), F32),
            pltpu.VMEM((2, 5, 8, 128), F32),
            pltpu.VMEM((2, 5, 8, 128), F32),
            pltpu.VMEM((6, 4, 8, 128), F32),
            pltpu.SemaphoreType.DMA((7,)),
            pltpu.SemaphoreType.DMA((11,)),
            pltpu.SemaphoreType.DMA((9,)),
            pltpu.SemaphoreType.REGULAR,
        ],
        compiler_params=pltpu.CompilerParams(
            collective_id=0, has_side_effects=True, vmem_limit_bytes=24 * 1024 * 1024
        ),
    )(*[pltpu.with_memory_space_constraint(x, pltpu.HBM) for x in (cell[0], count, frac[0], vel[0], mass[0], stress[0], drag)])
    frac_out, vel_out, stress_out = pl.pallas_call(
        particles_kernel,
        out_shape=[
            jax.ShapeDtypeStruct((3, 64, 128), F32),
            jax.ShapeDtypeStruct((3, 64, 128), F32),
            jax.ShapeDtypeStruct((64, 128), F32),
        ],
        in_specs=[vmem] * len(passed),
        out_specs=[anywhere] * 3,
        scratch_shapes=[
            pltpu.VMEM((3, 64, 128), F32),
            pltpu.VMEM((3, 64, 128), F32),
            pltpu.VMEM((64, 128), F32),
            pltpu.VMEM((8, 256, 128), F32),
            pltpu.SemaphoreType.DMA((3,)),
        ],
        compiler_params=pltpu.CompilerParams(vmem_limit_bytes=24 * 1024 * 1024),
    )(*state)
    return frac_out[None], vel_out[None], stress_out[None]


def solution(mesh):
    in_specs = (
        P("phase", "space", None),
        P("phase", "space"),
        P("phase", None, "space", None),
        P("phase", None, "space", None),
        P("phase", "space", None),
        P("phase", "space", None),
        P("space", None, None),
    )
    out_specs = (
        P("phase", None, "space", None),
        P("phase", None, "space", None),
        P("phase", "space", None),
    )
    return jax.shard_map(local, mesh=mesh, in_specs=in_specs, out_specs=out_specs, check_vma=False)
```

```python
import jax
import jax.numpy as jnp
from jax import lax
from jax.experimental import pallas as pl
from jax.experimental.pallas import tpu as pltpu
from jax.sharding import PartitionSpec as P

F32 = jnp.float32
BF16 = jnp.bfloat16
DT = 0.05
MESH = pl.DeviceIdType.MESH
RUN = 32
ROW = 8

FX, MASS, QX, QY, QZ, S2 = 0, 6, 7, 8, 9, 10
NROW = 11


def split(value):
    high = value.astype(BF16)
    low = (value - high.astype(F32)).astype(BF16)
    return high, low


def factors(frac):
    r = frac - 0.5
    return 0.5 * (0.5 - r) * (0.5 - r), 0.75 - r * r, 0.5 * (0.5 + r) * (0.5 + r)


def coords(cell_ref, frac, j):
    here = pl.ds(8 * j, 8)
    cell = cell_ref[here, :]
    cx = cell >> 4
    cy = (cell >> 2) & 3
    cz = cell & 3
    by = j // 4
    pos_x = cx.astype(F32) + (frac[0, here, :] - 2.0)
    pos_y = (cy + 4 * by).astype(F32) + (frac[1, here, :] - 4.0)
    return here, cx, cy, cz, by, pos_x, pos_y


def gather(vt_s, ph_s, pl_s, fz_s, fzt_s, red_s, cell_ref, live_s, state, out):
    frac, vel, stress = state
    frac_out, vel_out, stress_out = out
    sub8 = lax.broadcasted_iota(jnp.int32, (8, 128), 0)

    def body(i):
        for par in range(2):
            bz = 2 * i + par
            window = []
            for c in range(4):
                here = vt_s[c, pl.ds(pl.multiple_of(8 * i + 8, 8), 8), :]
                if par == 0:
                    beside = vt_s[c, pl.ds(pl.multiple_of(8 * i, 8), 8), :]
                    window.append(jnp.where(sub8 == 7, beside, here))
                else:
                    beside = vt_s[c, pl.ds(pl.multiple_of(8 * i + 16, 8), 8), :]
                    window.append(jnp.where(sub8 == 0, beside, here))
            window = jnp.concatenate(window, axis=0).astype(BF16)
            high, low, none = ph_s[bz], pl_s[bz], jnp.zeros((32, 256), BF16)
            got = jnp.dot(
                jnp.concatenate([window, window], axis=1),
                jnp.concatenate([high, high, none, low, low, none], axis=0),
                preferred_element_type=F32,
            )
            at = pl.ds(pl.multiple_of(8 * bz, 8), 8)
            for by in range(2):
                fz, fzt = fz_s[by, at, :], fzt_s[by, at, :]
                u = [got[8 * c : 8 * c + 8, 128 * by : 128 * by + 128] for c in range(4)]
                for c in range(3):
                    red_s[2 * c + by, at, :] = fz * u[c]
                red_s[6 + by, at, :] = fz * u[3] + fzt * u[2]

    def finish(j):
        here, cx, cy, cz, by, pos_x, pos_y = coords(cell_ref, frac, j)
        sums = []
        for c in range(4):
            parts = [red_s[2 * c + by, pl.ds(64 * (j % 4) + s, 8, stride=8), :] for s in range(8)]
            while len(parts) > 1:
                parts = [parts[k] + parts[k + 1] for k in range(0, len(parts), 2)]
            sums.append(parts[0])
        live = live_s[here, :] > 0.5
        rate = sums[3] - pos_x * sums[0] - pos_y * sums[1] - (frac[2, here, :] - 0.5) * sums[2]
        stress_out[here, :] = stress[here, :] - jnp.where(live, (4.0 * 4.0 * DT) * rate, 0.0)
        for e in range(3):
            f = frac[e, here, :]
            frac_out[e, here, :] = jnp.where(live, f + DT * sums[e], f)
            vel_out[e, here, :] = jnp.where(live, sums[e], vel[e, here, :])

    for chunk in range(4):
        for i in range(4 * chunk, 4 * chunk + 4):
            body(i)
        finish(chunk)
        finish(chunk + 4)


def nodes_kernel(
    cell_hbm,
    count_hbm,
    frac_hbm,
    vel_hbm,
    mass_hbm,
    stress_hbm,
    drag_hbm,
    cell_ref,
    live_s,
    frac_mid,
    vel_mid,
    stress_mid,
    ph_s,
    pl_s,
    fz_s,
    fzt_s,
    vt_s,
    count_ref,
    frac_in,
    vel_in,
    mass_ref,
    stress_in,
    drag_ref,
    rows_s,
    fy_s,
    even_s,
    odd_s,
    red_s,
    grid_s,
    edge_s,
    left_s,
    right_s,
    cross_left_s,
    cross_right_s,
    other_s,
    load_sem,
    send_sem,
    recv_sem,
    open_sem,
):
    n_space = lax.axis_size("space")
    me = lax.axis_index("space")
    phase = lax.axis_index("phase")
    right = lax.rem(me + 1, n_space)
    left = lax.rem(me + n_space - 1, n_space)
    to_left = (left, phase)
    to_right = (right, phase)
    to_other = (me, 1 - phase)
    to_cross_left = (left, 1 - phase)
    to_cross_right = (right, 1 - phase)

    has_left = me > 0
    has_right = me < n_space - 1
    run_left = lax.rem(me, RUN) == 0
    run_right = lax.rem(me, RUN) == RUN - 1
    cross_left = jnp.logical_and(has_left, run_left)
    cross_right = jnp.logical_and(has_right, run_right)
    relay_left = jnp.logical_and(cross_left, phase == 0)
    relay_right = jnp.logical_and(cross_right, phase == 0)
    direct_left = jnp.logical_and(has_left, jnp.logical_not(jnp.logical_and(run_left, phase == 1)))
    direct_right = jnp.logical_and(has_right, jnp.logical_not(jnp.logical_and(run_right, phase == 1)))
    row_left = jnp.logical_and(lax.rem(me, ROW) == 0, jnp.logical_not(run_left))
    row_right = jnp.logical_and(lax.rem(me, ROW) == ROW - 1, jnp.logical_not(run_right))
    raw_out_left = jnp.logical_or(run_left, jnp.logical_and(row_left, phase == 1))
    raw_out_right = jnp.logical_or(run_right, jnp.logical_and(row_right, phase == 1))
    out_left = jnp.logical_and(has_left, raw_out_left)
    out_right = jnp.logical_and(has_right, raw_out_right)
    in_left = jnp.logical_or(cross_left, jnp.logical_and(row_left, phase == 0))
    in_right = jnp.logical_or(cross_right, jnp.logical_and(row_right, phase == 0))
    barrier = pltpu.get_barrier_semaphore()

    def greet(target, sem=barrier):
        pl.semaphore_signal(sem, inc=1, device_id=target, device_id_type=MESH)

    def greet_across():
        greet(to_other)
        pl.when(in_left)(lambda: greet(to_cross_left))
        pl.when(in_right)(lambda: greet(to_cross_right))

    def answer_across():
        greet(to_other, open_sem)
        pl.when(cross_left)(lambda: greet(to_cross_left, open_sem))
        pl.when(cross_right)(lambda: greet(to_cross_right, open_sem))

    def enter():
        pl.semaphore_wait(barrier, greeted)
        answer_across()

    def count(*flags):
        return sum(flag.astype(jnp.int32) for flag in flags)

    pl.when(direct_left)(lambda: greet(to_left))
    pl.when(direct_right)(lambda: greet(to_right))
    pl.when(phase == 0)(greet_across)
    greeted = count(direct_left, direct_right) + phase * (1 + count(out_left, out_right))
    answered = 1 + count(cross_left, cross_right)

    loads = [
        pltpu.make_async_copy(src, dst, load_sem.at[k])
        for k, (src, dst) in enumerate(
            (
                (frac_hbm, frac_in),
                (cell_hbm, cell_ref),
                (count_hbm, count_ref),
                (vel_hbm, vel_in),
                (mass_hbm, mass_ref),
                (stress_hbm, stress_in),
                (drag_hbm, drag_ref),
            )
        )
    ]
    for load in loads:
        load.start()

    def remote(src, dst, sem, target, arrival=None):
        return pltpu.make_async_remote_copy(
            src_ref=src,
            dst_ref=dst,
            send_sem=send_sem.at[sem],
            recv_sem=recv_sem.at[sem if arrival is None else arrival],
            device_id=target,
            device_id_type=MESH,
        )

    sub8 = lax.broadcasted_iota(jnp.int32, (8, 128), 0)
    zero8 = jnp.zeros((8, 128), F32)
    for c in range(5):
        even_s[c, 128:136, :] = zero8
        odd_s[c, 0:8, :] = zero8
    fy_s[...] = jnp.zeros((2, 256, 128), F32)
    for c in range(4):
        vt_s[c, 0:8, :] = zero8
        vt_s[c, 136:144, :] = zero8

    for load in loads:
        load.wait()

    diagonal = lax.broadcasted_iota(jnp.int32, (64, 64), 0) == lax.broadcasted_iota(jnp.int32, (64, 64), 1)
    counts = jnp.broadcast_to(count_ref[...].astype(F32), (64, 64))
    counts = jnp.sum(jnp.where(diagonal, counts, 0.0), axis=1, keepdims=True)
    slots = lax.broadcasted_iota(jnp.int32, (64, 128), 1).astype(F32)
    live_s[...] = jnp.where(slots < counts, 1.0, 0.0)

    def prepare(chunk, frac, vel, stress):
        for j in (chunk, chunk + 4):
            here, cx, cy, cz, by, pos_x, pos_y = coords(cell_ref, frac, j)
            wx = factors(frac[0, here, :])
            wy = factors(frac[1, here, :])
            wz = factors(frac[2, here, :])
            on_x = [cx == k for k in range(4)]
            on_y = [cy == k for k in range(4)]
            on_z = [cz == k for k in range(4)]

            def place(on, w, node):
                value = zero8
                for k in range(4):
                    if 0 <= node - k <= 2 and w[node - k] is not None:
                        value = jnp.where(on[k], w[node - k], value)
                return value

            for a in range(6):
                rows_s[FX + a, here, :] = place(on_x, wx, a)
            start = 64 * (j % 4)
            for node in range(6):
                y = 4 * by + node - 1
                if 0 <= y < 8:
                    fy_s[by, pl.ds(start + y, 8, stride=8), :] = place(on_y, wy, node)
            tz = (-wz[0], None, wz[2])
            for ref, w in ((fz_s, wz), (fzt_s, tz)):
                nodes = [place(on_z, w, node) for node in range(6)] + [zero8, zero8]
                for r in range(8):
                    value = jnp.where((sub8 & 1) == 0, nodes[(r + 1) % 8], nodes[(r + 5) % 8])
                    ref[by, pl.ds(start + r, 8, stride=8), :] = value
            live = live_s[here, :] > 0.5
            m = jnp.where(live, mass_ref[here, :], 0.0)
            s2 = jnp.where(live, stress[here, :], 0.0) * (4.0 * DT)
            rows_s[MASS, here, :] = m
            rows_s[S2, here, :] = s2
            rows_s[QX, here, :] = m * vel[0, here, :] - s2 * pos_x
            rows_s[QY, here, :] = m * vel[1, here, :] - s2 * pos_y
            rows_s[QZ, here, :] = m * vel[2, here, :] - s2 * (frac[2, here, :] - 0.5)

    def deposit(step, state):
        def body(i):
            for par in range(2):
                bz = 2 * i + par
                plane = []
                column = []
                for by in range(2):
                    at = pl.ds(bz + 32 * by, 1)

                    def row(f):
                        return jnp.broadcast_to(rows_s[f, at, :], (8, 128))

                    here = pl.ds(pl.multiple_of(8 * bz, 8), 8)
                    fy = fy_s[by, here, :]
                    fz = fz_s[by, here, :]
                    s2 = row(S2)
                    plane.append(jnp.concatenate([row(FX + a) * fy for a in range(6)], axis=0))
                    column.append(
                        jnp.concatenate(
                            [
                                row(MASS) * fz,
                                row(QX) * fz,
                                row(QY) * fz,
                                row(QZ) * fz + s2 * fzt_s[by, here, :],
                                s2 * fz,
                            ],
                            axis=0,
                        )
                    )
                plane_hi, plane_lo = split(jnp.concatenate(plane, axis=1))
                ph_s[bz] = plane_hi
                pl_s[bz] = plane_lo
                column_hi, column_lo = split(jnp.concatenate(column, axis=1))
                out = lax.dot_general(
                    jnp.concatenate([column_hi, column_lo], axis=0),
                    jnp.concatenate([plane_hi, plane_lo, jnp.zeros((32, 256), BF16)], axis=0),
                    (((1,), (1,)), ((), ())),
                    preferred_element_type=F32,
                )
                out = out[:40] + out[40:]
                for c in range(5):
                    if par == 0:
                        even_s[c, pl.ds(pl.multiple_of(8 * i, 8), 8), :] = out[8 * c : 8 * c + 8]
                    else:
                        odd_s[c, pl.ds(pl.multiple_of(8 * i + 8, 8), 8), :] = out[8 * c : 8 * c + 8]

        for chunk in range(4):
            if step == 0 and chunk == 2:
                pl.when(phase == 1)(enter)
            prepare(chunk, *state)
            for i in range(4 * chunk, 4 * chunk + 4):
                body(i)
        fields = []
        row7 = (lax.broadcasted_iota(jnp.int32, (128, 128), 0) & 7) == 7
        row0 = (lax.broadcasted_iota(jnp.int32, (128, 128), 0) & 7) == 0
        for c in range(5):
            total = jnp.where(row7, even_s[c, 8:136, :], even_s[c, 0:128, :]) + jnp.where(
                row0, odd_s[c, 0:128, :], odd_s[c, 8:136, :]
            )
            turned = total.T
            fields.append((turned[0:48] + turned[48:96]).reshape(6, 8, 128))
        y = sub8.astype(F32) - 3.5
        for a in range(6):
            grid_s[step, a, 0] = fields[0][a]
            grid_s[step, a, 1] = fields[1][a] + (a - 2.5) * fields[4][a]
            grid_s[step, a, 2] = fields[2][a] + y * fields[4][a]
            grid_s[step, a, 3] = fields[3][a]

    floor = lax.broadcasted_iota(jnp.int32, (8, 128), 1) == 0

    def velocity(mass, momentum):
        inverse = 1.0 / jnp.maximum(mass, 0.25)
        v = [momentum[e] * inverse for e in range(3)]
        v[2] = v[2] - DT
        v[2] = jnp.where(floor, jnp.maximum(v[2], 0.0), v[2])
        return v

    def turn(node_vel):
        y = sub8.astype(F32) - 3.5
        for c in range(4):
            if c < 3:
                values = [node_vel[a][c] for a in range(6)]
            else:
                values = [(a - 2.5) * node_vel[a][0] + y * node_vel[a][1] for a in range(6)]
            values = jnp.concatenate(values, axis=0)
            high = values.astype(BF16).astype(F32)
            turned = jnp.concatenate([high, values - high, jnp.zeros((32, 128), F32)], axis=0).T
            vt_s[c, 8:136, :] = turned

    def settled(a, c, mine, from_left, from_right, use_left, use_right):
        if a < 2:
            return mine[a, c] + jnp.where(use_left, from_left[a, c], 0.0)
        if a < 4:
            return mine[a, c]
        return mine[a, c] + jnp.where(use_right, from_right[a - 4, c], 0.0)

    started = []

    def own(a, step):
        mine = grid_s.at[step]
        full = [settled(a, c, mine, left_s.at[step], right_s.at[step], has_left, has_right) for c in range(4)]
        return full[0], velocity(full[0], full[1:])

    for step in range(2):
        state = (frac_in, vel_in, stress_in) if step == 0 else (frac_mid, vel_mid, stress_mid)
        deposit(step, state)
        mine = grid_s.at[step]
        width = 5 if step == 0 else 4
        leftward = remote(mine.at[0:2, 0:width], right_s.at[step, :, 0:width], 2 * step, to_left)
        rightward = remote(mine.at[4:6, 0:width], left_s.at[step, :, 0:width], 2 * step + 1, to_right)
        go_left, go_right = (direct_left, direct_right) if step == 0 else (has_left, has_right)
        started += [(go_left, leftward), (go_right, rightward)]
        if step == 0:
            for a in range(1, 5):
                mine[a, 4] = drag_ref[a - 1]
            mine[0, 4] = zero8
            mine[5, 4] = zero8
            pl.when(phase == 0)(lambda: pl.semaphore_wait(barrier, greeted))
        if step == 0:
            inner = remote(mine.at[2:4, 0:4], other_s.at[2:4], 4, to_other)
            pl.when(phase == 1)(inner.start)
        pl.when(go_left)(leftward.start)
        pl.when(go_right)(rightward.start)
        node = {a: own(a, step) for a in (2, 3)}
        if step == 0:
            cross_leftward = remote(mine.at[0:2], cross_right_s, 5, to_cross_left)
            cross_rightward = remote(mine.at[4:6], cross_left_s, 6, to_cross_right)
            raw_left = remote(mine.at[0:2, 0:4], other_s.at[0:2], 7, to_other)
            raw_right = remote(mine.at[4:6, 0:4], other_s.at[4:6], 8, to_other)
            sum_left = remote(edge_s.at[0:2], other_s.at[0:2], 7, to_other)
            sum_right = remote(edge_s.at[2:4], other_s.at[4:6], 8, to_other)

            def begin_across():
                pl.semaphore_wait(open_sem, answered)
                inner.start()

            pl.when(phase == 0)(begin_across)

            def send_raw(flag, run, cross, raw):
                pl.when(flag)(cross.start)
                pl.when(run)(raw.start)

            send_raw(out_left, raw_out_left, cross_leftward, raw_left)
            send_raw(out_right, raw_out_right, cross_rightward, raw_right)
            started += [(out_left, cross_leftward), (out_right, cross_rightward)]
            started += [(None, inner), (None, sum_left), (None, sum_right)]

            def send_sum_left():
                rightward.wait_recv()
                for a in range(2):
                    for c in range(4):
                        edge_s[a, c] = mine[a, c] + left_s[0, a, c]
                sum_left.start()

            def send_sum_right():
                leftward.wait_recv()
                for a in range(2):
                    for c in range(4):
                        edge_s[2 + a, c] = mine[4 + a, c] + right_s[0, a, c]
                sum_right.start()

            near_left = lax.rem(me, 2) == 1
            pl.when(near_left)(send_sum_left)
            pl.when(jnp.logical_not(raw_out_right))(send_sum_right)
            pl.when(jnp.logical_not(jnp.logical_or(near_left, raw_out_left)))(send_sum_left)
            pass_left = remote(cross_left_s, left_s.at[0], 9, to_other, 1)
            pass_right = remote(cross_right_s, right_s.at[0], 10, to_other, 0)
            started += [(relay_left, pass_left), (relay_right, pass_right)]

            def pass_on(cross, onward):
                cross.wait_recv()
                onward.start()

            pl.when(relay_left)(lambda: pass_on(cross_rightward, pass_left))
            pl.when(relay_right)(lambda: pass_on(cross_leftward, pass_right))
            pl.when(out_left)(rightward.wait_recv)
            pl.when(out_right)(leftward.wait_recv)
            for a in (0, 1, 4, 5):
                node[a] = own(a, step)
            inner.wait_recv()
            pl.when(jnp.logical_and(in_left, jnp.logical_not(relay_left)))(cross_rightward.wait_recv)
            pl.when(jnp.logical_and(in_right, jnp.logical_not(relay_right)))(cross_leftward.wait_recv)
            sum_left.wait_recv()
            sum_right.wait_recv()
        else:
            pl.when(has_left)(rightward.wait_recv)
            pl.when(has_right)(leftward.wait_recv)
            for a in (0, 1, 4, 5):
                node[a] = own(a, step)
        node_vel = []
        for a in range(6):
            mass, v = node[a]
            if step == 0:
                other = [settled(a, c, other_s, cross_left_s, cross_right_s, in_left, in_right) for c in range(4)]
                other_vel = velocity(other[0], other[1:])
                coef = left_s[0, 0, 4] if a == 0 else right_s[0, 1, 4] if a == 5 else drag_ref[a - 1]
                slip = [other_vel[e] - v[e] for e in range(3)]
                rate = coef * jnp.sqrt(slip[0] * slip[0] + slip[1] * slip[1] + slip[2] * slip[2] + 0.25)
                gain = rate / (1.0 + rate) * (other[0] / (mass + other[0] + 0.25))
                v = [v[e] + gain * slip[e] for e in range(3)]
            if a == 0:
                v = [jnp.where(has_left, value, 0.0) for value in v]
            if a == 5:
                v = [jnp.where(has_right, value, 0.0) for value in v]
            node_vel.append(v)
        turn(node_vel)
        if step == 0:
            gather(
                vt_s, ph_s, pl_s, fz_s, fzt_s, red_s, cell_ref, live_s, state, (frac_mid, vel_mid, stress_mid)
            )
    for flag, copy in started:
        if flag is None:
            copy.wait_send()
        else:
            pl.when(flag)(copy.wait_send)


def particles_kernel(
    cell_ref,
    live_s,
    frac_mid,
    vel_mid,
    stress_mid,
    ph_s,
    pl_s,
    fz_s,
    fzt_s,
    vt_s,
    frac_hbm,
    vel_hbm,
    stress_hbm,
    frac_out,
    vel_out,
    stress_out,
    red_s,
    store_sem,
):
    gather(
        vt_s,
        ph_s,
        pl_s,
        fz_s,
        fzt_s,
        red_s,
        cell_ref,
        live_s,
        (frac_mid, vel_mid, stress_mid),
        (frac_out, vel_out, stress_out),
    )
    stores = [
        pltpu.make_async_copy(src, dst, store_sem.at[k])
        for k, (src, dst) in enumerate(((frac_out, frac_hbm), (vel_out, vel_hbm), (stress_out, stress_hbm)))
    ]
    for store in stores:
        store.start()
    for store in stores:
        store.wait()


def local(cell, count, frac, vel, mass, stress, drag):
    vmem = pl.BlockSpec(memory_space=pltpu.VMEM)
    anywhere = pl.BlockSpec(memory_space=pl.ANY)
    passed = [
        ((64, 128), jnp.int32),
        ((64, 128), F32),
        ((3, 64, 128), F32),
        ((3, 64, 128), F32),
        ((64, 128), F32),
        ((32, 48, 256), BF16),
        ((32, 48, 256), BF16),
        ((2, 256, 128), F32),
        ((2, 256, 128), F32),
        ((4, 144, 128), F32),
    ]
    state = pl.pallas_call(
        nodes_kernel,
        out_shape=[jax.ShapeDtypeStruct(shape, kind) for shape, kind in passed],
        in_specs=[anywhere] * 7,
        out_specs=[vmem] * len(passed),
        scratch_shapes=[
            pltpu.VMEM((1, 64), jnp.int32),
            pltpu.VMEM((3, 64, 128), F32),
            pltpu.VMEM((3, 64, 128), F32),
            pltpu.VMEM((64, 128), F32),
            pltpu.VMEM((64, 128), F32),
            pltpu.VMEM((4, 8, 128), F32),
            pltpu.VMEM((NROW, 64, 128), F32),
            pltpu.VMEM((2, 256, 128), F32),
            pltpu.VMEM((5, 136, 128), F32),
            pltpu.VMEM((5, 136, 128), F32),
            pltpu.VMEM((8, 256, 128), F32),
            pltpu.VMEM((2, 6, 5, 8, 128), F32),
            pltpu.VMEM((4, 4, 8, 128), F32),
            pltpu.VMEM((2, 2, 5, 8, 128), F32),
            pltpu.VMEM((2, 2, 5, 8, 128), F32),
            pltpu.VMEM((2, 5, 8, 128), F32),
            pltpu.VMEM((2, 5, 8, 128), F32),
            pltpu.VMEM((6, 4, 8, 128), F32),
            pltpu.SemaphoreType.DMA((7,)),
            pltpu.SemaphoreType.DMA((11,)),
            pltpu.SemaphoreType.DMA((9,)),
            pltpu.SemaphoreType.REGULAR,
        ],
        compiler_params=pltpu.CompilerParams(
            collective_id=0, has_side_effects=True, vmem_limit_bytes=24 * 1024 * 1024
        ),
    )(*[pltpu.with_memory_space_constraint(x, pltpu.HBM) for x in (cell[0], count, frac[0], vel[0], mass[0], stress[0], drag)])
    frac_out, vel_out, stress_out = pl.pallas_call(
        particles_kernel,
        out_shape=[
            jax.ShapeDtypeStruct((3, 64, 128), F32),
            jax.ShapeDtypeStruct((3, 64, 128), F32),
            jax.ShapeDtypeStruct((64, 128), F32),
        ],
        in_specs=[vmem] * len(passed),
        out_specs=[anywhere] * 3,
        scratch_shapes=[
            pltpu.VMEM((3, 64, 128), F32),
            pltpu.VMEM((3, 64, 128), F32),
            pltpu.VMEM((64, 128), F32),
            pltpu.VMEM((8, 256, 128), F32),
            pltpu.SemaphoreType.DMA((3,)),
        ],
        compiler_params=pltpu.CompilerParams(vmem_limit_bytes=24 * 1024 * 1024),
    )(*state)
    return frac_out[None], vel_out[None], stress_out[None]


def solution(mesh):
    in_specs = (
        P("phase", "space", None),
        P("phase", "space"),
        P("phase", None, "space", None),
        P("phase", None, "space", None),
        P("phase", "space", None),
        P("phase", "space", None),
        P("space", None, None),
    )
    out_specs = (
        P("phase", None, "space", None),
        P("phase", None, "space", None),
        P("phase", "space", None),
    )
    return jax.shard_map(local, mesh=mesh, in_specs=in_specs, out_specs=out_specs, check_vma=False)
```

```python
import jax
import jax.numpy as jnp
from jax import lax
from jax.experimental import pallas as pl
from jax.experimental.pallas import tpu as pltpu
from jax.sharding import PartitionSpec as P

F32 = jnp.float32
BF16 = jnp.bfloat16
DT = 0.05
MESH = pl.DeviceIdType.MESH
RUN = 32

FX, MASS, QX, QY, QZ, S2 = 0, 6, 7, 8, 9, 10
NROW = 11


def split(value):
    high = value.astype(BF16)
    low = (value - high.astype(F32)).astype(BF16)
    return high, low


def factors(frac):
    r = frac - 0.5
    return 0.5 * (0.5 - r) * (0.5 - r), 0.75 - r * r, 0.5 * (0.5 + r) * (0.5 + r)


def coords(cell_ref, frac, j):
    here = pl.ds(8 * j, 8)
    cell = cell_ref[here, :]
    cx = cell >> 4
    cy = (cell >> 2) & 3
    cz = cell & 3
    by = j // 4
    pos_x = cx.astype(F32) + (frac[0, here, :] - 2.0)
    pos_y = (cy + 4 * by).astype(F32) + (frac[1, here, :] - 4.0)
    return here, cx, cy, cz, by, pos_x, pos_y


def gather(vt_s, ph_s, pl_s, fz_s, fzt_s, red_s, cell_ref, live_s, state, out):
    frac, vel, stress = state
    frac_out, vel_out, stress_out = out
    sub8 = lax.broadcasted_iota(jnp.int32, (8, 128), 0)

    def body(i):
        for par in range(2):
            bz = 2 * i + par
            window = []
            for c in range(4):
                here = vt_s[c, pl.ds(pl.multiple_of(8 * i + 8, 8), 8), :]
                if par == 0:
                    beside = vt_s[c, pl.ds(pl.multiple_of(8 * i, 8), 8), :]
                    window.append(jnp.where(sub8 == 7, beside, here))
                else:
                    beside = vt_s[c, pl.ds(pl.multiple_of(8 * i + 16, 8), 8), :]
                    window.append(jnp.where(sub8 == 0, beside, here))
            window = jnp.concatenate(window, axis=0).astype(BF16)
            high, low, none = ph_s[bz], pl_s[bz], jnp.zeros((32, 256), BF16)
            got = jnp.dot(
                jnp.concatenate([window, window], axis=1),
                jnp.concatenate([high, high, none, low, low, none], axis=0),
                preferred_element_type=F32,
            )
            at = pl.ds(pl.multiple_of(8 * bz, 8), 8)
            for by in range(2):
                fz, fzt = fz_s[by, at, :], fzt_s[by, at, :]
                u = [got[8 * c : 8 * c + 8, 128 * by : 128 * by + 128] for c in range(4)]
                for c in range(3):
                    red_s[2 * c + by, at, :] = fz * u[c]
                red_s[6 + by, at, :] = fz * u[3] + fzt * u[2]

    def finish(j):
        here, cx, cy, cz, by, pos_x, pos_y = coords(cell_ref, frac, j)
        sums = []
        for c in range(4):
            parts = [red_s[2 * c + by, pl.ds(64 * (j % 4) + s, 8, stride=8), :] for s in range(8)]
            while len(parts) > 1:
                parts = [parts[k] + parts[k + 1] for k in range(0, len(parts), 2)]
            sums.append(parts[0])
        live = live_s[here, :] > 0.5
        rate = sums[3] - pos_x * sums[0] - pos_y * sums[1] - (frac[2, here, :] - 0.5) * sums[2]
        stress_out[here, :] = stress[here, :] - jnp.where(live, (4.0 * 4.0 * DT) * rate, 0.0)
        for e in range(3):
            f = frac[e, here, :]
            frac_out[e, here, :] = jnp.where(live, f + DT * sums[e], f)
            vel_out[e, here, :] = jnp.where(live, sums[e], vel[e, here, :])

    for chunk in range(4):
        for i in range(4 * chunk, 4 * chunk + 4):
            body(i)
        finish(chunk)
        finish(chunk + 4)


def nodes_kernel(
    cell_hbm,
    count_hbm,
    frac_hbm,
    vel_hbm,
    mass_hbm,
    stress_hbm,
    drag_hbm,
    cell_ref,
    live_s,
    frac_mid,
    vel_mid,
    stress_mid,
    ph_s,
    pl_s,
    fz_s,
    fzt_s,
    vt_s,
    count_ref,
    frac_in,
    vel_in,
    mass_ref,
    stress_in,
    drag_ref,
    rows_s,
    fy_s,
    even_s,
    odd_s,
    red_s,
    grid_s,
    edge_s,
    left_s,
    right_s,
    cross_left_s,
    cross_right_s,
    other_s,
    load_sem,
    send_sem,
    recv_sem,
):
    n_space = lax.axis_size("space")
    me = lax.axis_index("space")
    phase = lax.axis_index("phase")
    right = lax.rem(me + 1, n_space)
    left = lax.rem(me + n_space - 1, n_space)
    to_left = (left, phase)
    to_right = (right, phase)
    to_other = (me, 1 - phase)
    to_cross_left = (left, 1 - phase)
    to_cross_right = (right, 1 - phase)

    has_left = me > 0
    has_right = me < n_space - 1
    run_left = lax.rem(me, RUN) == 0
    run_right = lax.rem(me, RUN) == RUN - 1
    cross_left = jnp.logical_and(has_left, run_left)
    cross_right = jnp.logical_and(has_right, run_right)
    relay_left = jnp.logical_and(cross_left, phase == 0)
    relay_right = jnp.logical_and(cross_right, phase == 0)
    direct_left = jnp.logical_and(has_left, jnp.logical_not(jnp.logical_and(run_left, phase == 1)))
    direct_right = jnp.logical_and(has_right, jnp.logical_not(jnp.logical_and(run_right, phase == 1)))
    barrier = pltpu.get_barrier_semaphore()

    def greet(target):
        pl.semaphore_signal(barrier, inc=1, device_id=target, device_id_type=MESH)

    greet(to_other)
    pl.when(direct_left)(lambda: greet(to_left))
    pl.when(direct_right)(lambda: greet(to_right))
    pl.when(cross_left)(lambda: greet(to_cross_left))
    pl.when(cross_right)(lambda: greet(to_cross_right))
    greeted = 1 + sum(flag.astype(jnp.int32) for flag in (direct_left, direct_right, cross_left, cross_right))

    loads = [
        pltpu.make_async_copy(src, dst, load_sem.at[k])
        for k, (src, dst) in enumerate(
            (
                (frac_hbm, frac_in),
                (cell_hbm, cell_ref),
                (count_hbm, count_ref),
                (vel_hbm, vel_in),
                (mass_hbm, mass_ref),
                (stress_hbm, stress_in),
                (drag_hbm, drag_ref),
            )
        )
    ]
    for load in loads:
        load.start()

    def remote(src, dst, sem, target, arrival=None):
        return pltpu.make_async_remote_copy(
            src_ref=src,
            dst_ref=dst,
            send_sem=send_sem.at[sem],
            recv_sem=recv_sem.at[sem if arrival is None else arrival],
            device_id=target,
            device_id_type=MESH,
        )

    sub8 = lax.broadcasted_iota(jnp.int32, (8, 128), 0)
    zero8 = jnp.zeros((8, 128), F32)
    for c in range(5):
        even_s[c, 128:136, :] = zero8
        odd_s[c, 0:8, :] = zero8
    fy_s[...] = jnp.zeros((2, 256, 128), F32)
    for c in range(4):
        vt_s[c, 0:8, :] = zero8
        vt_s[c, 136:144, :] = zero8

    for load in loads:
        load.wait()

    diagonal = lax.broadcasted_iota(jnp.int32, (64, 64), 0) == lax.broadcasted_iota(jnp.int32, (64, 64), 1)
    counts = jnp.broadcast_to(count_ref[...].astype(F32), (64, 64))
    counts = jnp.sum(jnp.where(diagonal, counts, 0.0), axis=1, keepdims=True)
    slots = lax.broadcasted_iota(jnp.int32, (64, 128), 1).astype(F32)
    live_s[...] = jnp.where(slots < counts, 1.0, 0.0)

    def prepare(chunk, frac, vel, stress):
        for j in (chunk, chunk + 4):
            here, cx, cy, cz, by, pos_x, pos_y = coords(cell_ref, frac, j)
            wx = factors(frac[0, here, :])
            wy = factors(frac[1, here, :])
            wz = factors(frac[2, here, :])
            on_x = [cx == k for k in range(4)]
            on_y = [cy == k for k in range(4)]
            on_z = [cz == k for k in range(4)]

            def place(on, w, node):
                value = zero8
                for k in range(4):
                    if 0 <= node - k <= 2 and w[node - k] is not None:
                        value = jnp.where(on[k], w[node - k], value)
                return value

            for a in range(6):
                rows_s[FX + a, here, :] = place(on_x, wx, a)
            start = 64 * (j % 4)
            for node in range(6):
                y = 4 * by + node - 1
                if 0 <= y < 8:
                    fy_s[by, pl.ds(start + y, 8, stride=8), :] = place(on_y, wy, node)
            tz = (-wz[0], None, wz[2])
            for ref, w in ((fz_s, wz), (fzt_s, tz)):
                nodes = [place(on_z, w, node) for node in range(6)] + [zero8, zero8]
                for r in range(8):
                    value = jnp.where((sub8 & 1) == 0, nodes[(r + 1) % 8], nodes[(r + 5) % 8])
                    ref[by, pl.ds(start + r, 8, stride=8), :] = value
            live = live_s[here, :] > 0.5
            m = jnp.where(live, mass_ref[here, :], 0.0)
            s2 = jnp.where(live, stress[here, :], 0.0) * (4.0 * DT)
            rows_s[MASS, here, :] = m
            rows_s[S2, here, :] = s2
            rows_s[QX, here, :] = m * vel[0, here, :] - s2 * pos_x
            rows_s[QY, here, :] = m * vel[1, here, :] - s2 * pos_y
            rows_s[QZ, here, :] = m * vel[2, here, :] - s2 * (frac[2, here, :] - 0.5)

    def deposit(step, state):
        def body(i):
            for par in range(2):
                bz = 2 * i + par
                plane = []
                column = []
                for by in range(2):
                    at = pl.ds(bz + 32 * by, 1)

                    def row(f):
                        return jnp.broadcast_to(rows_s[f, at, :], (8, 128))

                    here = pl.ds(pl.multiple_of(8 * bz, 8), 8)
                    fy = fy_s[by, here, :]
                    fz = fz_s[by, here, :]
                    s2 = row(S2)
                    plane.append(jnp.concatenate([row(FX + a) * fy for a in range(6)], axis=0))
                    column.append(
                        jnp.concatenate(
                            [
                                row(MASS) * fz,
                                row(QX) * fz,
                                row(QY) * fz,
                                row(QZ) * fz + s2 * fzt_s[by, here, :],
                                s2 * fz,
                            ],
                            axis=0,
                        )
                    )
                plane_hi, plane_lo = split(jnp.concatenate(plane, axis=1))
                ph_s[bz] = plane_hi
                pl_s[bz] = plane_lo
                column_hi, column_lo = split(jnp.concatenate(column, axis=1))
                out = lax.dot_general(
                    jnp.concatenate([column_hi, column_lo], axis=0),
                    jnp.concatenate([plane_hi, plane_lo, jnp.zeros((32, 256), BF16)], axis=0),
                    (((1,), (1,)), ((), ())),
                    preferred_element_type=F32,
                )
                out = out[:40] + out[40:]
                for c in range(5):
                    if par == 0:
                        even_s[c, pl.ds(pl.multiple_of(8 * i, 8), 8), :] = out[8 * c : 8 * c + 8]
                    else:
                        odd_s[c, pl.ds(pl.multiple_of(8 * i + 8, 8), 8), :] = out[8 * c : 8 * c + 8]

        for chunk in range(4):
            prepare(chunk, *state)
            for i in range(4 * chunk, 4 * chunk + 4):
                body(i)
        fields = []
        row7 = (lax.broadcasted_iota(jnp.int32, (128, 128), 0) & 7) == 7
        row0 = (lax.broadcasted_iota(jnp.int32, (128, 128), 0) & 7) == 0
        for c in range(5):
            total = jnp.where(row7, even_s[c, 8:136, :], even_s[c, 0:128, :]) + jnp.where(
                row0, odd_s[c, 0:128, :], odd_s[c, 8:136, :]
            )
            turned = total.T
            fields.append((turned[0:48] + turned[48:96]).reshape(6, 8, 128))
        y = sub8.astype(F32) - 3.5
        for a in range(6):
            grid_s[step, a, 0] = fields[0][a]
            grid_s[step, a, 1] = fields[1][a] + (a - 2.5) * fields[4][a]
            grid_s[step, a, 2] = fields[2][a] + y * fields[4][a]
            grid_s[step, a, 3] = fields[3][a]

    floor = lax.broadcasted_iota(jnp.int32, (8, 128), 1) == 0

    def velocity(mass, momentum):
        inverse = 1.0 / jnp.maximum(mass, 0.25)
        v = [momentum[e] * inverse for e in range(3)]
        v[2] = v[2] - DT
        v[2] = jnp.where(floor, jnp.maximum(v[2], 0.0), v[2])
        return v

    def turn(node_vel):
        y = sub8.astype(F32) - 3.5
        for c in range(4):
            if c < 3:
                values = [node_vel[a][c] for a in range(6)]
            else:
                values = [(a - 2.5) * node_vel[a][0] + y * node_vel[a][1] for a in range(6)]
            values = jnp.concatenate(values, axis=0)
            high = values.astype(BF16).astype(F32)
            turned = jnp.concatenate([high, values - high, jnp.zeros((32, 128), F32)], axis=0).T
            vt_s[c, 8:136, :] = turned

    def settled(a, c, mine, from_left, from_right, use_left, use_right):
        if a < 2:
            return mine[a, c] + jnp.where(use_left, from_left[a, c], 0.0)
        if a < 4:
            return mine[a, c]
        return mine[a, c] + jnp.where(use_right, from_right[a - 4, c], 0.0)

    started = []

    def own(a, step):
        mine = grid_s.at[step]
        full = [settled(a, c, mine, left_s.at[step], right_s.at[step], has_left, has_right) for c in range(4)]
        return full[0], velocity(full[0], full[1:])

    for step in range(2):
        state = (frac_in, vel_in, stress_in) if step == 0 else (frac_mid, vel_mid, stress_mid)
        deposit(step, state)
        mine = grid_s.at[step]
        width = 5 if step == 0 else 4
        leftward = remote(mine.at[0:2, 0:width], right_s.at[step, :, 0:width], 2 * step, to_left)
        rightward = remote(mine.at[4:6, 0:width], left_s.at[step, :, 0:width], 2 * step + 1, to_right)
        go_left, go_right = (direct_left, direct_right) if step == 0 else (has_left, has_right)
        started += [(go_left, leftward), (go_right, rightward)]
        if step == 0:
            for a in range(1, 5):
                mine[a, 4] = drag_ref[a - 1]
            mine[0, 4] = zero8
            mine[5, 4] = zero8
            pl.semaphore_wait(barrier, greeted)
        if step == 0:
            inner = remote(mine.at[2:4, 0:4], other_s.at[2:4], 4, to_other)
            inner.start()
        pl.when(go_left)(leftward.start)
        pl.when(go_right)(rightward.start)
        node = {a: own(a, step) for a in (2, 3)}
        if step == 0:
            cross_leftward = remote(mine.at[0:2], cross_right_s, 5, to_cross_left)
            cross_rightward = remote(mine.at[4:6], cross_left_s, 6, to_cross_right)
            raw_left = remote(mine.at[0:2, 0:4], other_s.at[0:2], 7, to_other)
            raw_right = remote(mine.at[4:6, 0:4], other_s.at[4:6], 8, to_other)
            sum_left = remote(edge_s.at[0:2], other_s.at[0:2], 7, to_other)
            sum_right = remote(edge_s.at[2:4], other_s.at[4:6], 8, to_other)

            def send_raw(flag, run, cross, raw):
                pl.when(flag)(cross.start)
                pl.when(run)(raw.start)

            send_raw(cross_left, run_left, cross_leftward, raw_left)
            send_raw(cross_right, run_right, cross_rightward, raw_right)
            started += [(cross_left, cross_leftward), (cross_right, cross_rightward)]
            started += [(None, inner), (None, sum_left), (None, sum_right)]

            def send_sum_left():
                rightward.wait_recv()
                for a in range(2):
                    for c in range(4):
                        edge_s[a, c] = mine[a, c] + left_s[0, a, c]
                sum_left.start()

            def send_sum_right():
                leftward.wait_recv()
                for a in range(2):
                    for c in range(4):
                        edge_s[2 + a, c] = mine[4 + a, c] + right_s[0, a, c]
                sum_right.start()

            near_left = lax.rem(me, 2) == 1
            pl.when(near_left)(send_sum_left)
            pl.when(jnp.logical_not(run_right))(send_sum_right)
            pl.when(jnp.logical_not(jnp.logical_or(near_left, run_left)))(send_sum_left)
            pass_left = remote(cross_left_s, left_s.at[0], 9, to_other, 1)
            pass_right = remote(cross_right_s, right_s.at[0], 10, to_other, 0)
            started += [(relay_left, pass_left), (relay_right, pass_right)]

            def pass_on(cross, onward):
                cross.wait_recv()
                onward.start()

            pl.when(relay_left)(lambda: pass_on(cross_rightward, pass_left))
            pl.when(relay_right)(lambda: pass_on(cross_leftward, pass_right))
            pl.when(cross_left)(rightward.wait_recv)
            pl.when(cross_right)(leftward.wait_recv)
            for a in (0, 1, 4, 5):
                node[a] = own(a, step)
            inner.wait_recv()
            pl.when(jnp.logical_and(cross_left, phase == 1))(cross_rightward.wait_recv)
            pl.when(jnp.logical_and(cross_right, phase == 1))(cross_leftward.wait_recv)
            sum_left.wait_recv()
            sum_right.wait_recv()
        else:
            pl.when(has_left)(rightward.wait_recv)
            pl.when(has_right)(leftward.wait_recv)
            for a in (0, 1, 4, 5):
                node[a] = own(a, step)
        node_vel = []
        for a in range(6):
            mass, v = node[a]
            if step == 0:
                other = [settled(a, c, other_s, cross_left_s, cross_right_s, cross_left, cross_right) for c in range(4)]
                other_vel = velocity(other[0], other[1:])
                coef = left_s[0, 0, 4] if a == 0 else right_s[0, 1, 4] if a == 5 else drag_ref[a - 1]
                slip = [other_vel[e] - v[e] for e in range(3)]
                rate = coef * jnp.sqrt(slip[0] * slip[0] + slip[1] * slip[1] + slip[2] * slip[2] + 0.25)
                gain = rate / (1.0 + rate) * (other[0] / (mass + other[0] + 0.25))
                v = [v[e] + gain * slip[e] for e in range(3)]
            if a == 0:
                v = [jnp.where(has_left, value, 0.0) for value in v]
            if a == 5:
                v = [jnp.where(has_right, value, 0.0) for value in v]
            node_vel.append(v)
        turn(node_vel)
        if step == 0:
            gather(
                vt_s, ph_s, pl_s, fz_s, fzt_s, red_s, cell_ref, live_s, state, (frac_mid, vel_mid, stress_mid)
            )
    for flag, copy in started:
        if flag is None:
            copy.wait_send()
        else:
            pl.when(flag)(copy.wait_send)


def particles_kernel(
    cell_ref,
    live_s,
    frac_mid,
    vel_mid,
    stress_mid,
    ph_s,
    pl_s,
    fz_s,
    fzt_s,
    vt_s,
    frac_hbm,
    vel_hbm,
    stress_hbm,
    frac_out,
    vel_out,
    stress_out,
    red_s,
    store_sem,
):
    gather(
        vt_s,
        ph_s,
        pl_s,
        fz_s,
        fzt_s,
        red_s,
        cell_ref,
        live_s,
        (frac_mid, vel_mid, stress_mid),
        (frac_out, vel_out, stress_out),
    )
    stores = [
        pltpu.make_async_copy(src, dst, store_sem.at[k])
        for k, (src, dst) in enumerate(((frac_out, frac_hbm), (vel_out, vel_hbm), (stress_out, stress_hbm)))
    ]
    for store in stores:
        store.start()
    for store in stores:
        store.wait()


def local(cell, count, frac, vel, mass, stress, drag):
    vmem = pl.BlockSpec(memory_space=pltpu.VMEM)
    anywhere = pl.BlockSpec(memory_space=pl.ANY)
    passed = [
        ((64, 128), jnp.int32),
        ((64, 128), F32),
        ((3, 64, 128), F32),
        ((3, 64, 128), F32),
        ((64, 128), F32),
        ((32, 48, 256), BF16),
        ((32, 48, 256), BF16),
        ((2, 256, 128), F32),
        ((2, 256, 128), F32),
        ((4, 144, 128), F32),
    ]
    state = pl.pallas_call(
        nodes_kernel,
        out_shape=[jax.ShapeDtypeStruct(shape, kind) for shape, kind in passed],
        in_specs=[anywhere] * 7,
        out_specs=[vmem] * len(passed),
        scratch_shapes=[
            pltpu.VMEM((1, 64), jnp.int32),
            pltpu.VMEM((3, 64, 128), F32),
            pltpu.VMEM((3, 64, 128), F32),
            pltpu.VMEM((64, 128), F32),
            pltpu.VMEM((64, 128), F32),
            pltpu.VMEM((4, 8, 128), F32),
            pltpu.VMEM((NROW, 64, 128), F32),
            pltpu.VMEM((2, 256, 128), F32),
            pltpu.VMEM((5, 136, 128), F32),
            pltpu.VMEM((5, 136, 128), F32),
            pltpu.VMEM((8, 256, 128), F32),
            pltpu.VMEM((2, 6, 5, 8, 128), F32),
            pltpu.VMEM((4, 4, 8, 128), F32),
            pltpu.VMEM((2, 2, 5, 8, 128), F32),
            pltpu.VMEM((2, 2, 5, 8, 128), F32),
            pltpu.VMEM((2, 5, 8, 128), F32),
            pltpu.VMEM((2, 5, 8, 128), F32),
            pltpu.VMEM((6, 4, 8, 128), F32),
            pltpu.SemaphoreType.DMA((7,)),
            pltpu.SemaphoreType.DMA((11,)),
            pltpu.SemaphoreType.DMA((9,)),
        ],
        compiler_params=pltpu.CompilerParams(
            collective_id=0, has_side_effects=True, vmem_limit_bytes=24 * 1024 * 1024
        ),
    )(*[pltpu.with_memory_space_constraint(x, pltpu.HBM) for x in (cell[0], count, frac[0], vel[0], mass[0], stress[0], drag)])
    frac_out, vel_out, stress_out = pl.pallas_call(
        particles_kernel,
        out_shape=[
            jax.ShapeDtypeStruct((3, 64, 128), F32),
            jax.ShapeDtypeStruct((3, 64, 128), F32),
            jax.ShapeDtypeStruct((64, 128), F32),
        ],
        in_specs=[vmem] * len(passed),
        out_specs=[anywhere] * 3,
        scratch_shapes=[
            pltpu.VMEM((3, 64, 128), F32),
            pltpu.VMEM((3, 64, 128), F32),
            pltpu.VMEM((64, 128), F32),
            pltpu.VMEM((8, 256, 128), F32),
            pltpu.SemaphoreType.DMA((3,)),
        ],
        compiler_params=pltpu.CompilerParams(vmem_limit_bytes=24 * 1024 * 1024),
    )(*state)
    return frac_out[None], vel_out[None], stress_out[None]


def solution(mesh):
    in_specs = (
        P("phase", "space", None),
        P("phase", "space"),
        P("phase", None, "space", None),
        P("phase", None, "space", None),
        P("phase", "space", None),
        P("phase", "space", None),
        P("space", None, None),
    )
    out_specs = (
        P("phase", None, "space", None),
        P("phase", None, "space", None),
        P("phase", "space", None),
    )
    return jax.shard_map(local, mesh=mesh, in_specs=in_specs, out_specs=out_specs, check_vma=False)
```
